128 devices in a mesh: sec: 16 (over x, y), ctx: 8 (over z, core).
Axes of the slice: x: 4, y: 4, z: 4, core: 2. Of those that a mesh axis runs over, the one named last changes fastest.
Arguments:
- patches: bfloat16 [32, 256, 5120], P(None, ('sec', 'ctx')), may hold values from -6 to 6
- patch_gain: float32 [1280], replicated, may hold values from 0.5 to 1.5
- w_merge_in: bfloat16 [5120, 5120], P(None, 'ctx'), may hold values from -0.078125 to 0.078125
- b_merge_in: float32 [5120], P('ctx'), may hold values from -3 to 3
- w_merge_out: bfloat16 [5120, 8192], P('ctx'), may hold values from -0.078125 to 0.078125
- b_merge_out: float32 [8192], replicated, may hold values from -3 to 3
- text_embed: bfloat16 [16, 1024, 8192], P('sec', 'ctx'), may hold values from -6 to 6
- norm_gain: float32 [8192], replicated, may hold values from 0.5 to 1.5
- upstream: bfloat16 [16, 1024, 8192], P('sec', 'ctx'), may hold values from -6 to 6
- img_seq: int32 [256], replicated, may hold values from 0 to 15, as said below
- img_off: int32 [256], replicated, may hold values from 0 to 1016, as said below
- img_cnt: int32 [256], replicated, may hold values from 8 to 32, as said below
Outputs:
- normed: bfloat16 [16, 1024, 8192], P('sec', 'ctx')
- image_grad: bfloat16 [32, 256, 8192], P(None, ('sec', 'ctx'))
The draws below stay inside these ranges and needn't reach their ends.
Inputs may be any that keep to these rules, and one draw needn't show every extreme that they name: `img_seq`: the 16 images of one index of sec (a block of 16 consecutive image numbers) go to 16 different sequences. Image g occupies positions img_off[g] to img_off[g] + img_cnt[g] - 1 of sequence img_seq[g]; images never intersect, and each aligned block of 128 positions of a sequence holds exactly 2 whole images. Slots from img_cnt[g] on are padding.
All inputs are finite; a program needn't handle non-finite values.
Results may differ from the reference program's by a relative error of at most 0.011.
Values may be sent and summed in bfloat16 or wider, within the bound.
A program may use at most 128 MiB of HBM per device.

```python
import jax
import jax.numpy as jnp
from jax import lax

D = 8192
VIS = 1280
MERGE = 4
VH = 5120
CAP = 32
S_DEV = 128
SEQS = 16
IMG_DEV = 2
NIMG = 256
L = 1024
SUB = 64
N_CTX = 8


def image_layout(key):
    key_list = jax.random.split(key, 5)
    targets = jax.vmap(lambda sub_key: jax.random.permutation(sub_key, SEQS))(jax.random.split(key_list[0], SEQS)).astype(jnp.int32)
    arrival = jax.vmap(lambda sub_key: jax.random.permutation(sub_key, SEQS))(jax.random.split(key_list[1], SEQS)).astype(jnp.int32)
    lowest = max(1, CAP // 4)
    sources = jnp.arange(SEQS, dtype=jnp.int32)[:, None]
    placed = arrival[targets, sources]
    counts = jax.random.randint(key_list[2], (SEQS, SEQS), lowest, CAP + 1, dtype=jnp.int32)
    counts = jnp.where(placed == 0, CAP, counts)
    counts = jnp.where(placed == SEQS - 1, lowest, counts).astype(jnp.int32)
    spare_room = SUB - counts + 1
    shifts = jax.random.randint(key_list[4], (SEQS, SEQS), 0, 1 << 20, dtype=jnp.int32) % spare_room
    shifts = jnp.where(placed == 0, 0, shifts)
    shifts = jnp.where(placed == SEQS - 1, spare_room - 1, shifts)
    offsets = placed // IMG_DEV * S_DEV + placed % IMG_DEV * SUB + shifts
    return (targets.reshape(-1), offsets.reshape(-1).astype(jnp.int32), counts.reshape(-1))


def draw_img_seq(key, part):
    return image_layout(key)[0]


def draw_img_off(key, part):
    return image_layout(key)[1]


def draw_img_cnt(key, part):
    return image_layout(key)[2]


def level_of(key, shape, shards, smallest, top_value):
    gain, own = 1.0, jax.random.fold_in(key, 6)
    for position, shards_of in shards:
        draws = jnp.exp(jax.random.uniform(jax.random.fold_in(own, position), (shards_of,), jnp.float32, smallest / len(shards), top_value / len(shards)))
        gain = gain * jnp.repeat(draws, shape[position] // shards_of).reshape([-1 if axis == position else 1 for axis in range(len(shape))])
    return gain


def gaussian(own_key, extent, scale, limit, cuts=(), kind=jnp.bfloat16):
    array = scale * jax.random.normal(own_key, extent, jnp.float32)
    if cuts:
        array = array * level_of(own_key, extent, cuts, -0.22, 0.18)
    return jnp.clip(array, -limit, limit).astype(kind)


def setup_inputs(seed: int = 0) -> dict:
    seeds = jax.random.split(jax.random.key(seed), 13)
    return {
        "patches": gaussian(seeds[0], (CAP, NIMG, VH), 1.0, 6.0, ((1, 128),)),
        "patch_gain": jnp.clip(jax.random.uniform(seeds[1], (VIS,), jnp.float32, 0.5, 1.5), 0.5, 1.5),
        "w_merge_in": gaussian(seeds[2], (VH, VH), VH ** -0.5, 0.078125, ((1, 8),)),
        "b_merge_in": gaussian(seeds[3], (VH,), 0.5, 3.0, ((0, 8),), jnp.float32),
        "w_merge_out": gaussian(seeds[4], (VH, D), VH ** -0.5, 0.078125, ((0, 8),)),
        "b_merge_out": gaussian(seeds[5], (D,), 0.5, 3.0, (), jnp.float32),
        "text_embed": gaussian(seeds[6], (SEQS, L, D), 1.0, 6.0, ((0, 16), (1, 8))),
        "norm_gain": jnp.clip(jax.random.uniform(seeds[7], (D,), jnp.float32, 0.5, 1.5), 0.5, 1.5),
        "upstream": gaussian(seeds[8], (SEQS, L, D), 1.0, 6.0, ((0, 16), (1, 8))),
        "img_seq": draw_img_seq(jax.random.fold_in(seeds[12], 71), 0),
        "img_off": draw_img_off(jax.random.fold_in(seeds[12], 71), 0),
        "img_cnt": draw_img_cnt(jax.random.fold_in(seeds[12], 71), 0),
    }


def reference(patches, patch_gain, w_merge_in, b_merge_in, w_merge_out, b_merge_out, text_embed, norm_gain, upstream, img_seq, img_off, img_cnt):
    features = patches.astype(jnp.float32).reshape(CAP, NIMG, MERGE, VIS)
    inverse = lax.rsqrt(lax.optimization_barrier(jnp.mean(features * features, axis=-1, keepdims=True)) + 1e-06)
    normed_patches = (features * inverse * patch_gain).reshape(CAP, NIMG, VH).astype(jnp.bfloat16)
    pre_act = jnp.dot(normed_patches, w_merge_in, preferred_element_type=jnp.float32) + b_merge_in
    merger_hidden = jax.nn.gelu(pre_act, approximate=False).astype(jnp.bfloat16)
    block_width = VH // N_CTX
    accumulated = jnp.zeros((CAP, NIMG, D), jnp.float32)
    for portion in range(N_CTX):
        partial_sum = jnp.dot(merger_hidden[:, :, portion * block_width:(portion + 1) * block_width], w_merge_out[portion * block_width:(portion + 1) * block_width], preferred_element_type=jnp.float32)
        accumulated = accumulated + lax.optimization_barrier(partial_sum.astype(jnp.bfloat16)).astype(jnp.float32)
    image_embed = (accumulated + b_merge_out).astype(jnp.bfloat16)
    slot_iota = jnp.arange(CAP, dtype=jnp.int32)[:, None]
    valid_slot = slot_iota < img_cnt[None, :]
    flat_index = img_seq[None, :] * L + img_off[None, :] + slot_iota
    target_index = jnp.where(valid_slot, flat_index, SEQS * L).astype(jnp.int32)
    embeds = text_embed.reshape(SEQS * L, D).at[target_index.reshape(-1)].set(image_embed.reshape(CAP * NIMG, D), mode='drop')
    values = embeds.astype(jnp.float32)
    inv_rms = lax.rsqrt(lax.optimization_barrier(jnp.mean(values * values, axis=-1, keepdims=True)) + 1e-06)
    normed = (values * inv_rms * norm_gain).astype(jnp.bfloat16).reshape(SEQS, L, D)
    scaled_upstream = upstream.reshape(SEQS * L, D).astype(jnp.float32) * norm_gain
    inner_mean = lax.optimization_barrier(jnp.mean(values * scaled_upstream, axis=-1, keepdims=True))
    embed_grad = (inv_rms * scaled_upstream - values * inv_rms ** 3 * inner_mean).astype(jnp.bfloat16)
    source_index = jnp.where(valid_slot, flat_index, 0).astype(jnp.int32)
    picked = jnp.take(embed_grad, source_index.reshape(-1), axis=0).reshape(CAP, NIMG, D)
    image_grad = jnp.where(valid_slot[:, :, None], picked, jnp.zeros_like(picked))
    return (normed, image_grad)
```

```python
import jax
import jax.numpy as jnp
from jax import lax
from jax.sharding import PartitionSpec as P


def local(
    patches,
    patch_gain,
    w_merge_in,
    b_merge_in,
    w_merge_out,
    b_merge_out,
    text_embed,
    norm_gain,
    upstream,
    img_seq,
    img_off,
    img_cnt,
):
    slot_count, own_images, hidden_width = patches.shape
    vision_width = patch_gain.shape[0]
    sec_count = lax.axis_size("sec")
    seq_rows = text_embed.shape[1]
    sec_index = lax.axis_index("sec")
    ctx_index = lax.axis_index("ctx")
    iota_seq = jnp.arange(sec_count, dtype=jnp.int32)
    dest_table = img_seq.reshape(sec_count, sec_count)
    incoming = dest_table == sec_index
    offsets_in = jnp.sum(jnp.where(incoming, img_off.reshape(sec_count, sec_count), 0), axis=1)
    counts_in = jnp.sum(jnp.where(incoming, img_cnt.reshape(sec_count, sec_count), 0), axis=1)
    place = jnp.sum((offsets_in[None, :] < offsets_in[:, None]).astype(jnp.int32), axis=1)
    ordered = jnp.sum(
        jnp.where(place[None, :] == iota_seq[:, None], iota_seq[None, :], 0), axis=1
    )
    own_dest = lax.dynamic_index_in_dim(dest_table, sec_index, 0, keepdims=False)
    image_of_seq = jnp.sum(
        jnp.where(own_dest[None, :] == iota_seq[:, None], iota_seq[None, :], 0), axis=1
    )
    local_ids = lax.dynamic_slice_in_dim(ordered, ctx_index * own_images, own_images)
    first = jnp.take(offsets_in, local_ids) - ctx_index * seq_rows
    count = jnp.take(counts_in, local_ids)
    features = patches.astype(jnp.float32).reshape(
        slot_count, own_images, hidden_width // vision_width, vision_width
    )
    inverse = lax.rsqrt(jnp.mean(features * features, axis=-1, keepdims=True) + 1e-06)
    normed_patches = (
        (features * inverse * patch_gain)
        .reshape(slot_count, own_images, hidden_width)
        .astype(jnp.bfloat16)
        .transpose(1, 0, 2)
    )
    spread = lax.all_to_all(normed_patches, "ctx", split_axis=2, concat_axis=0, tiled=True)
    arrived = lax.all_to_all(jnp.take(spread, image_of_seq, axis=0), "sec", 0, 0, tiled=True)
    part = jnp.take(arrived, ordered, axis=0)
    group_patches = lax.all_gather(part, "ctx", axis=2, tiled=True).reshape(-1, hidden_width)
    pre_act = jnp.dot(group_patches, w_merge_in, preferred_element_type=jnp.float32) + b_merge_in
    hidden = jax.nn.gelu(pre_act, approximate=False).astype(jnp.bfloat16)
    summed = lax.psum_scatter(
        jnp.dot(hidden, w_merge_out, preferred_element_type=jnp.float32).astype(jnp.bfloat16),
        "ctx",
        scatter_dimension=0,
        tiled=True,
    ).astype(jnp.float32)
    image_rows = (summed + b_merge_out).astype(jnp.bfloat16)
    slots = jnp.arange(slot_count, dtype=jnp.int32)
    target = jnp.where(slots[None, :] < count[:, None], first[:, None] + slots[None, :], -1)
    pick = target.reshape(-1)[:, None] == jnp.arange(seq_rows, dtype=jnp.int32)[None, :]
    pick_rows = pick.astype(jnp.bfloat16)
    placed = jnp.dot(pick_rows.T, image_rows, preferred_element_type=jnp.float32)
    values = jnp.where(jnp.any(pick, axis=0)[:, None], placed, text_embed[0].astype(jnp.float32))
    inv_rms = lax.rsqrt(jnp.mean(values * values, axis=-1, keepdims=True) + 1e-06)
    normed = (values * inv_rms * norm_gain).astype(jnp.bfloat16)
    scaled_upstream = upstream[0].astype(jnp.float32) * norm_gain
    inner_mean = jnp.mean(values * scaled_upstream, axis=-1, keepdims=True)
    embed_grad = (inv_rms * scaled_upstream - values * inv_rms**3 * inner_mean).astype(jnp.bfloat16)
    slot_grad = jnp.dot(pick_rows, embed_grad, preferred_element_type=jnp.float32)
    slot_grad = slot_grad.astype(jnp.bfloat16).reshape(own_images, slot_count, -1)
    back = lax.all_to_all(slot_grad, "ctx", split_axis=2, concat_axis=0, tiled=True)
    home = lax.all_to_all(jnp.take(back, place, axis=0), "sec", 0, 0, tiled=True)
    own = lax.all_to_all(
        jnp.take(home, own_dest, axis=0), "ctx", split_axis=0, concat_axis=2, tiled=True
    )
    return (normed[None], own.transpose(1, 0, 2))


def solution(mesh):
    placed = (
        P(None, ("sec", "ctx"), None),
        P(),
        P(None, "ctx"),
        P("ctx"),
        P("ctx", None),
        P(),
        P("sec", "ctx", None),
        P(),
        P("sec", "ctx", None),
        P(),
        P(),
        P(),
    )
    return jax.shard_map(
        local,
        mesh=mesh,
        in_specs=placed,
        out_specs=(P("sec", "ctx", None), P(None, ("sec", "ctx"), None)),
        check_vma=False,
    )
```

```python
import jax
import jax.numpy as jnp
from jax import lax
from jax.experimental import pallas as pl
from jax.experimental.pallas import tpu as pltpu
from jax.sharding import PartitionSpec as P

MESH = pl.DeviceIdType.MESH
F32 = jnp.float32
BF = jnp.bfloat16
SIDE = 4
SUBS = 2
HALF = 16
TILE = 512
RING = 4


def kernel(
    tab,
    patches,
    patch_gain,
    b_in,
    b_out,
    gain,
    w_in_hbm,
    w_out_hbm,
    text_hbm,
    up_hbm,
    normed_hbm,
    grad_hbm,
    w_in,
    w_own,
    w_sib,
    text,
    up,
    xn,
    xr,
    ys,
    yr,
    xbuf,
    acc,
    hid,
    hid_sib,
    sums,
    far_s,
    far_r,
    near_s,
    near_r,
    v_s,
    v,
    sus,
    nrm,
    stat,
    gs,
    gr,
    hs,
    hr,
    os_,
    or_,
    loc,
    s_zs,
    r_zs,
    s_xy,
    r_xy,
    s_ag,
    r_ag,
    s_fw,
    r_fw,
    s_sib,
    r_sib,
    s_w,
    r_w,
    s_h,
    r_h,
    s_far,
    r_far,
    s_near,
    r_near,
    s_v,
    r_v,
    s_b1,
    r_b1,
    s_b2,
    r_b2,
    s_b3,
    r_b3,
):
    sec = lax.axis_index("sec")
    ctx = lax.axis_index("ctx")
    x, y = sec // SIDE, sec % SIDE
    z, k = ctx // 2, ctx % 2
    n_ctx = 2 * SIDE
    n_sec = SIDE * SIDE
    width = xn.shape[-1]
    tiles = far_s.shape[0]
    pieces = sus.shape[0]

    def at_ctx(c):
        return {"sec": sec, "ctx": c}

    def at_sec(s):
        return {"sec": s, "ctx": ctx}

    def plane_peer(d):
        return ((x + d // SIDE) % SIDE) * SIDE + (y + d % SIDE) % SIDE

    up_z = at_ctx(((z + 1) % SIDE) * 2 + k)
    down_z = at_ctx(((z + SIDE - 1) % SIDE) * 2 + k)
    sib = at_ctx(z * 2 + 1 - k)

    def remote(src, dst, ssem, rsem, device):
        return pltpu.make_async_remote_copy(
            src_ref=src,
            dst_ref=dst,
            send_sem=ssem,
            recv_sem=rsem,
            device_id=device,
            device_id_type=MESH,
        )

    cols = w_own.shape[1]
    load_up = pltpu.make_async_copy(up_hbm, up, loc.at[0])
    load_text = pltpu.make_async_copy(text_hbm, text, loc.at[1])
    load_in = pltpu.make_async_copy(w_in_hbm, w_in, loc.at[2])
    load_own = pltpu.make_async_copy(
        w_out_hbm.at[:, pl.ds(pl.multiple_of(k * cols, cols), cols)], w_own, loc.at[3]
    )

    barrier = pltpu.get_barrier_semaphore()

    def greet_ctx(d, carry):
        pl.semaphore_signal(
            barrier, inc=1, device_id=at_ctx((ctx + d) % n_ctx), device_id_type=MESH
        )
        return carry

    def greet_sec(d, carry):
        pl.semaphore_signal(barrier, inc=1, device_id=at_sec(plane_peer(d)), device_id_type=MESH)
        return carry

    lax.fori_loop(1, n_ctx, greet_ctx, 0)
    lax.fori_loop(1, n_sec, greet_sec, 0)
    load_up.start()
    load_text.start()
    load_in.start()
    load_own.start()

    groups = patches.shape[2] // patch_gain.shape[1]
    group = patch_gain.shape[1]
    for i in range(2):
        for g in range(groups):
            f = patches[:, i, pl.ds(g * group, group)].astype(F32)
            inv = lax.rsqrt(jnp.mean(f * f, axis=-1, keepdims=True) + 1e-06)
            f = (f * inv * patch_gain[...]).astype(BF)
            for b in range(group // width):
                for h in range(2):
                    xn[h, g * (group // width) + b, i] = f[
                        h * HALF : (h + 1) * HALF, b * width : (b + 1) * width
                    ]

    pl.semaphore_wait(barrier, n_ctx + n_sec - 2)

    for h in range(2):

        def send_spread(d, carry, h=h):
            c = (ctx + d) % n_ctx
            remote(xn.at[h, c], xr[h].at[ctx], s_zs.at[h], r_zs.at[h], at_ctx(c)).start()
            return carry

        lax.fori_loop(1, n_ctx, send_spread, 0)
        xr[h][ctx] = xn[h, ctx]
    send_w = remote(
        w_out_hbm.at[:, pl.ds(pl.multiple_of((1 - k) * cols, cols), cols)], w_sib, s_w, r_w, sib
    )

    for h in range(2):
        remote(
            xn.at[h, pl.ds(0, n_ctx - 1)], xr[h].at[pl.ds(0, n_ctx - 1)], s_zs.at[h], r_zs.at[h], sib
        ).wait_recv()

        def send_plane(d, carry, h=h):
            q = plane_peer(d)
            n = tab[0, q]
            ys[h, q] = xr[h][n // 2, n % 2]
            remote(ys.at[h, q], yr[h].at[sec], s_xy.at[h], r_xy.at[h], at_sec(q)).start()
            return carry

        lax.fori_loop(1, n_sec, send_plane, 0)
        n = tab[0, sec]
        yr[h][sec] = xr[h][n // 2, n % 2]
    send_w.start()

    first = [tab[4, 0], tab[4, 1]]
    count = [tab[4, 2], tab[4, 3]]
    rows = text.shape[0]

    def placement(shape, slot_axis, row_axis):
        r = lax.broadcasted_iota(jnp.int32, shape, slot_axis)
        p = lax.broadcasted_iota(jnp.int32, shape, row_axis)
        slot = (r // (2 * HALF)) * HALF + r % HALF
        second = (r // HALF) % 2 == 1
        start = jnp.where(second, first[1], first[0])
        length = jnp.where(second, count[1], count[0])
        return jnp.where((slot < length) & (p == start + slot), 1.0, 0.0).astype(BF)

    load_up.wait()
    pick = placement((4 * HALF, rows), 0, 1)

    def gather_upstream(j, carry):
        at = pl.ds(pl.multiple_of(j * TILE, TILE), TILE)
        sus[j] = jnp.dot(pick, up[:, at], preferred_element_type=F32).astype(BF)
        return carry

    lax.fori_loop(0, pieces, gather_upstream, 0)
    load_text.wait()

    def norm_text(b, carry):
        at = pl.ds(pl.multiple_of(b * HALF, HALF), HALF)
        t = text[at, :].astype(F32)
        inv = lax.rsqrt(jnp.mean(t * t, axis=-1, keepdims=True) + 1e-06)
        nrm[at, :] = (t * inv * gain[...]).astype(BF)
        return carry

    lax.fori_loop(0, rows // HALF, norm_text, 0)
    load_in.wait()

    def multiply(c, h, start=False):
        part = jnp.dot(
            xbuf[c, h],
            w_in[pl.ds(pl.multiple_of(c * width, width), width), :],
            preferred_element_type=F32,
        )
        acc[h] = part if start else acc[h] + part

    c_down = ((z + SIDE - 1) % SIDE) * 2 + k
    c_up = ((z + 1) % SIDE) * 2 + k
    c_far = ((z + 2) % SIDE) * 2 + k

    def to_up(c, h, ssem, rsem):
        return remote(xbuf.at[c, h], xbuf.at[c, h], ssem, rsem, up_z)

    def to_down(c, h, ssem, rsem):
        return remote(xbuf.at[c, h], xbuf.at[c, h], ssem, rsem, down_z)

    def to_sib(c, h, rel):
        return remote(xbuf.at[c, h], xbuf.at[c, h], s_sib.at[rel, h], r_sib.at[rel, h], sib)

    for h in range(2):
        remote(
            ys.at[h, pl.ds(0, n_sec - 1)], yr[h].at[pl.ds(0, n_sec - 1)], s_xy.at[h], r_xy.at[h], sib
        ).wait_recv()
        for i in range(n_sec):
            xbuf[ctx, h, pl.ds(i * HALF, HALF), :] = yr[h][tab[1, i]]
        to_up(ctx, h, s_ag.at[0, h], r_ag.at[0, h]).start()
        to_down(ctx, h, s_ag.at[1, h], r_ag.at[1, h]).start()
        to_sib(ctx, h, 0).start()
        multiply(ctx, h, start=True)

    def other(c):
        return c + 1 - 2 * k

    for h in range(2):
        to_up(c_down, h, s_ag.at[0, h], r_ag.at[0, h]).wait_recv()
        if h == 0:
            to_up(c_down, 0, s_fw.at[0], r_fw.at[0]).start()
        to_sib(c_down, h, 3).start()
        to_down(c_up, h, s_ag.at[1, h], r_ag.at[1, h]).wait_recv()
        if h == 1:
            to_down(c_up, 1, s_fw.at[1], r_fw.at[1]).start()
        to_sib(c_up, h, 1).start()
        to_sib(other(ctx), h, 0).wait_recv()
        multiply(other(ctx), h)
        multiply(c_down, h)
        multiply(c_up, h)
        to_sib(other(c_down), h, 3).wait_recv()
        multiply(other(c_down), h)
        to_sib(other(c_up), h, 1).wait_recv()
        multiply(other(c_up), h)
    for h in range(2):
        if h == 0:
            to_up(c_far, 0, s_fw.at[0], r_fw.at[0]).wait_recv()
        else:
            to_down(c_far, 1, s_fw.at[1], r_fw.at[1]).wait_recv()
        to_sib(c_far, h, 2).start()
        multiply(c_far, h)
    for h in range(2):
        to_sib(other(c_far), h, 2).wait_recv()
        multiply(other(c_far), h)

    def activate(e, carry):
        h, c = e // n_ctx, e % n_ctx
        pre = acc[h, pl.ds(pl.multiple_of(c * 2 * HALF, 2 * HALF), 2 * HALF), :] + b_in[...]
        act = 0.5 * pre * (1.0 + lax.erf(pre * (0.5**0.5)))
        rel = (c // 2 + SIDE - z) % SIDE
        hid[rel, c % 2, h] = act.astype(BF)
        return carry

    lax.fori_loop(0, 2 * n_ctx, activate, 0)
    send_h = remote(hid, hid_sib, s_h, r_h, sib)
    send_h.start()
    load_own.wait()
    send_w.wait_recv()
    send_h.wait_recv()

    def far(t, way):
        return remote(
            far_s.at[t, way],
            far_r.at[t, way],
            s_far.at[t, way],
            r_far.at[t, way],
            up_z if way == 0 else down_z,
        )

    def near(t, way):
        return remote(
            near_s.at[t, way],
            near_r.at[t, way],
            s_near.at[t, way],
            r_near.at[t, way],
            up_z if way == 0 else down_z,
        )

    def to_v(t):
        return remote(v_s.at[t], v.at[k * tiles + t], s_v.at[t], r_v.at[t], sib)

    def from_v(t):
        return remote(v_s.at[t], v.at[(1 - k) * tiles + t], s_v.at[t], r_v.at[t], sib)

    block = 4 * HALF

    def step(t, carry):
        @pl.when(t < tiles)
        def _():
            at = pl.ds(pl.multiple_of(t * TILE, TILE), TILE)
            total = jnp.dot(
                hid[...].reshape(-1, width), w_own[:, at], preferred_element_type=F32
            ) + jnp.dot(hid_sib[...].reshape(-1, width), w_sib[:, at], preferred_element_type=F32)
            sums[t % RING] = total.reshape(SIDE, 2, block, TILE)
            for way in range(2):
                far_s[t, way] = sums[t % RING, 2, way].astype(BF)
                far(t, way).start()

        @pl.when((t >= 1) & (t <= tiles))
        def _():
            u = t - 1
            for way, rel in ((0, 1), (1, 3)):
                far(u, way).wait_recv()
                near_s[u, way, way] = (
                    sums[u % RING, rel, way] + far_r[u, way].astype(F32)
                ).astype(BF)
                near_s[u, way, 1 - way] = sums[u % RING, rel, 1 - way].astype(BF)
                near(u, way).start()

        @pl.when(t >= 2)
        def _():
            u = t - 2
            near(u, 0).wait_recv()
            near(u, 1).wait_recv()
            at = pl.ds(pl.multiple_of((k * tiles + u) * TILE, TILE), TILE)

            def whole(p):
                return (
                    sums[u % RING, 0, p]
                    + near_r[u, 0, p].astype(F32)
                    + near_r[u, 1, p].astype(F32)
                    + b_out[:, at]
                ).astype(BF)

            v_s[u] = whole(1 - k)
            to_v(u).start()
            v[k * tiles + u] = whole(k)

        return carry

    lax.fori_loop(0, tiles + 2, step, 0)

    def arrive(t, carry):
        from_v(t).wait_recv()
        return carry

    lax.fori_loop(0, tiles, arrive, 0)

    model = pieces * TILE

    def sum_rows(j, carry):
        squares, inner = carry
        at = pl.ds(pl.multiple_of(j * TILE, TILE), TILE)
        val = v[j].astype(F32)
        scaled = sus[j].astype(F32) * gain[:, at]
        return (
            squares + jnp.sum(val * val, axis=-1, keepdims=True),
            inner + jnp.sum(val * scaled, axis=-1, keepdims=True),
        )

    zero = jnp.zeros((block, 1), F32)
    squares, inner = lax.fori_loop(0, pieces, sum_rows, (zero, zero))
    inv = lax.rsqrt(squares / model + 1e-06)
    pull = inv**3 * (inner / model)
    stat[0] = jnp.broadcast_to(inv, stat.shape[1:])
    stat[1] = jnp.broadcast_to(pull, stat.shape[1:])
    per = pieces // n_ctx // SUBS

    def spread_back(sub, c):
        return remote(gs.at[sub, c], gr[sub].at[ctx], s_b1.at[sub], r_b1.at[sub], at_ctx(c))

    for sub in range(SUBS):

        def send_back(d, carry, sub=sub):
            c = (ctx + d) % n_ctx
            for b in range(per):
                j = (c * SUBS + sub) * per + b
                at = pl.ds(pl.multiple_of(j * TILE, TILE), TILE)
                scaled = sus[j].astype(F32) * gain[:, at]
                out = stat[0, :, :1] * scaled - v[j].astype(F32) * stat[1, :, :1]
                gs[sub, c, :, :, :, b * TILE : (b + 1) * TILE] = (
                    out.astype(BF).reshape(2, 2, HALF, TILE)
                )
            spread_back(sub, c).start()
            return carry

        lax.fori_loop(1, n_ctx, send_back, 0)
        c = ctx
        for b in range(per):
            j = (c * SUBS + sub) * per + b
            at = pl.ds(pl.multiple_of(j * TILE, TILE), TILE)
            scaled = sus[j].astype(F32) * gain[:, at]
            out = stat[0, :, :1] * scaled - v[j].astype(F32) * stat[1, :, :1]
            gr[sub][c, :, :, :, b * TILE : (b + 1) * TILE] = (
                out.astype(BF).reshape(2, 2, HALF, TILE)
            )

    def put_images():
        put = placement((rows, block), 1, 0)
        p = lax.broadcasted_iota(jnp.int32, (rows, 1), 0)
        covered = ((p >= first[0]) & (p < first[0] + count[0])) | (
            (p >= first[1]) & (p < first[1] + count[1])
        )

        def body(j, carry):
            at = pl.ds(pl.multiple_of(j * TILE, TILE), TILE)
            image = (v[j].astype(F32) * stat[0, :, :1] * gain[:, at]).astype(BF)
            placed = jnp.dot(put, image, preferred_element_type=F32)
            nrm[:, at] = jnp.where(covered, placed, nrm[:, at].astype(F32)).astype(BF)
            return carry

        lax.fori_loop(0, pieces, body, 0)

    def exchange_back(sub):
        spread_sizes = pl.ds(0, n_ctx - 1)
        remote(
            gs.at[sub, spread_sizes], gr[sub].at[spread_sizes], s_b1.at[sub], r_b1.at[sub], sib
        ).wait_recv()

        def send(d, carry):
            s = plane_peer(d)
            n = tab[2, s]
            for h in range(2):
                hs[sub, s, h] = gr[sub][n // 2, h, n % 2]
            remote(hs.at[sub, s], hr[sub].at[sec], s_b2.at[sub], r_b2.at[sub], at_sec(s)).start()
            return carry

        lax.fori_loop(1, n_sec, send, 0)
        n = tab[2, sec]
        for h in range(2):
            hr[sub][sec, h] = gr[sub][n // 2, h, n % 2]

    def exchange_home(sub):
        plane_sizes = pl.ds(0, n_sec - 1)
        remote(
            hs.at[sub, plane_sizes], hr[sub].at[plane_sizes], s_b2.at[sub], r_b2.at[sub], sib
        ).wait_recv()

        def send(d, carry):
            c = (ctx + d) % n_ctx
            for i in range(2):
                for h in range(2):
                    os_[sub, c, h, i] = hr[sub][tab[3, 2 * c + i], h]
            remote(os_.at[sub, c], or_.at[sub, ctx], s_b3.at[sub], r_b3.at[sub], at_ctx(c)).start()
            return carry

        lax.fori_loop(1, n_ctx, send, 0)
        for i in range(2):
            for h in range(2):
                or_[sub, ctx, h, i] = hr[sub][tab[3, 2 * ctx + i], h]

    for sub in range(SUBS):
        exchange_back(sub)
    put_images()
    store_normed = pltpu.make_async_copy(nrm, normed_hbm, loc.at[4])
    store_normed.start()
    for sub in range(SUBS):
        exchange_home(sub)
    last = pl.ds(0, n_ctx - 1)
    stores = []
    for sub in range(SUBS):
        remote(
            os_.at[sub, last], or_.at[sub, last], s_b3.at[sub], r_b3.at[sub], sib
        ).wait_recv()
        store = pltpu.make_async_copy(or_.at[sub], grad_hbm.at[sub], loc.at[5 + sub])
        store.start()
        stores.append(store)

    for h in range(2):
        remote(xn.at[h, last], xr[h].at[last], s_zs.at[h], r_zs.at[h], sib).wait_send()
        plane = pl.ds(0, n_sec - 1)
        remote(ys.at[h, plane], yr[h].at[plane], s_xy.at[h], r_xy.at[h], sib).wait_send()
        to_up(ctx, h, s_ag.at[0, h], r_ag.at[0, h]).wait_send()
        to_down(ctx, h, s_ag.at[1, h], r_ag.at[1, h]).wait_send()
        for rel in range(SIDE):
            to_sib(ctx, h, rel).wait_send()
    to_up(c_down, 0, s_fw.at[0], r_fw.at[0]).wait_send()
    to_down(c_up, 1, s_fw.at[1], r_fw.at[1]).wait_send()
    send_w.wait_send()
    send_h.wait_send()

    def drain(t, carry):
        for way in range(2):
            far(t, way).wait_send()
            near(t, way).wait_send()
        to_v(t).wait_send()
        return carry

    lax.fori_loop(0, tiles, drain, 0)
    for sub in range(SUBS):
        plane = pl.ds(0, n_sec - 1)
        remote(gs.at[sub, last], gr[sub].at[last], s_b1.at[sub], r_b1.at[sub], sib).wait_send()
        remote(hs.at[sub, plane], hr[sub].at[plane], s_b2.at[sub], r_b2.at[sub], sib).wait_send()
        remote(os_.at[sub, last], or_.at[sub, last], s_b3.at[sub], r_b3.at[sub], sib).wait_send()
    store_normed.wait()
    for store in stores:
        store.wait()


def local(
    patches,
    patch_gain,
    w_merge_in,
    b_merge_in,
    w_merge_out,
    b_merge_out,
    text_embed,
    norm_gain,
    upstream,
    img_seq,
    img_off,
    img_cnt,
):
    slot_count, own_images, hidden_width = patches.shape
    n_sec = lax.axis_size("sec")
    n_ctx = lax.axis_size("ctx")
    seq_rows, model = text_embed.shape[1:]
    sec_index = lax.axis_index("sec")
    ctx_index = lax.axis_index("ctx")
    iota_seq = jnp.arange(n_sec, dtype=jnp.int32)
    dest_table = img_seq.reshape(n_sec, n_sec)
    incoming = dest_table == sec_index
    offsets_in = jnp.sum(jnp.where(incoming, img_off.reshape(n_sec, n_sec), 0), axis=1)
    counts_in = jnp.sum(jnp.where(incoming, img_cnt.reshape(n_sec, n_sec), 0), axis=1)
    place = jnp.sum((offsets_in[None, :] < offsets_in[:, None]).astype(jnp.int32), axis=1)
    at_place = place[None, :] == iota_seq[:, None]
    ordered = jnp.sum(jnp.where(at_place, iota_seq[None, :], 0), axis=1)
    own_dest = jnp.sum(jnp.where((iota_seq == sec_index)[:, None], dest_table, 0), axis=0)
    image_of_seq = jnp.sum(
        jnp.where(own_dest[None, :] == iota_seq[:, None], iota_seq[None, :], 0), axis=1
    )
    mine = [place == ctx_index * own_images + i for i in range(own_images)]
    firsts = [jnp.sum(jnp.where(m, offsets_in, 0)) - ctx_index * seq_rows for m in mine]
    counts = [jnp.sum(jnp.where(m, counts_in, 0)) for m in mine]
    spans = jnp.stack(firsts + counts + [jnp.int32(0)] * (n_sec - 4))
    tab = jnp.stack([image_of_seq, ordered, place, own_dest, spans])

    width = hidden_width // n_ctx
    hidden = w_merge_in.shape[1]
    cols = model // 2
    tiles = cols // TILE
    pieces = model // TILE
    wide = model // n_ctx // SUBS
    block = 4 * HALF
    vmem = pl.BlockSpec(memory_space=pltpu.VMEM)
    hbm = pl.BlockSpec(memory_space=pl.ANY)
    dma = pltpu.SemaphoreType.DMA
    normed, grads = pl.pallas_call(
        kernel,
        out_shape=(
            jax.ShapeDtypeStruct((seq_rows, model), BF),
            jax.ShapeDtypeStruct((SUBS, n_ctx, 2, 2, HALF, wide), BF),
        ),
        in_specs=[pl.BlockSpec(memory_space=pltpu.SMEM)] + [vmem] * 5 + [hbm] * 4,
        out_specs=(hbm, hbm),
        scratch_shapes=[
            pltpu.VMEM((hidden_width, hidden), BF),
            pltpu.VMEM((hidden, cols), BF),
            pltpu.VMEM((hidden, cols), BF),
            pltpu.VMEM((seq_rows, model), BF),
            pltpu.VMEM((seq_rows, model), BF),
            pltpu.VMEM((2, n_ctx, 2, HALF, width), BF),
            [pltpu.VMEM((n_ctx, 2, HALF, width), BF)] * 2,
            pltpu.VMEM((2, n_sec, HALF, width), BF),
            [pltpu.VMEM((n_sec, HALF, width), BF)] * 2,
            pltpu.VMEM((n_ctx, 2, n_sec * HALF, width), BF),
            pltpu.VMEM((2, n_sec * HALF, hidden), F32),
            pltpu.VMEM((SIDE, 2, 2, 2 * HALF, hidden), BF),
            pltpu.VMEM((SIDE, 2, 2, 2 * HALF, hidden), BF),
            pltpu.VMEM((RING, SIDE, 2, block, TILE), F32),
            pltpu.VMEM((tiles, 2, block, TILE), BF),
            pltpu.VMEM((tiles, 2, block, TILE), BF),
            pltpu.VMEM((tiles, 2, 2, block, TILE), BF),
            pltpu.VMEM((tiles, 2, 2, block, TILE), BF),
            pltpu.VMEM((tiles, block, TILE), BF),
            pltpu.VMEM((pieces, block, TILE), BF),
            pltpu.VMEM((pieces, block, TILE), BF),
            pltpu.VMEM((seq_rows, model), BF),
            pltpu.VMEM((2, block, 128), F32),
            pltpu.VMEM((SUBS, n_ctx, 2, 2, HALF, wide), BF),
            [pltpu.VMEM((n_ctx, 2, 2, HALF, wide), BF)] * SUBS,
            pltpu.VMEM((SUBS, n_sec, 2, HALF, wide), BF),
            [pltpu.VMEM((n_sec, 2, HALF, wide), BF)] * SUBS,
            pltpu.VMEM((SUBS, n_ctx, 2, 2, HALF, wide), BF),
            pltpu.VMEM((SUBS, n_ctx, 2, 2, HALF, wide), BF),
            dma((5 + SUBS,)),
            dma((2,)),
            dma((2,)),
            dma((2,)),
            dma((2,)),
            dma((2, 2)),
            dma((2, 2)),
            dma((2,)),
            dma((2,)),
            dma((SIDE, 2)),
            dma((SIDE, 2)),
            dma,
            dma,
            dma,
            dma,
            dma((tiles, 2)),
            dma((tiles, 2)),
            dma((tiles, 2)),
            dma((tiles, 2)),
            dma((tiles,)),
            dma((tiles,)),
            dma((SUBS,)),
            dma((SUBS,)),
            dma((SUBS,)),
            dma((SUBS,)),
            dma((SUBS,)),
            dma((SUBS,)),
        ],
        compiler_params=pltpu.CompilerParams(
            collective_id=0, has_side_effects=True, vmem_limit_bytes=63 << 20
        ),
        name="merger",
    )(
        tab,
        patches,
        patch_gain.reshape(1, -1),
        b_merge_in.reshape(1, -1),
        b_merge_out.reshape(1, -1),
        norm_gain.reshape(1, -1),
        w_merge_in,
        w_merge_out,
        text_embed[0],
        upstream[0],
    )
    image_grad = grads.transpose(2, 4, 3, 1, 0, 5).reshape(slot_count, own_images, model)
    return (normed[None], image_grad)


def solution(mesh):
    placed = (
        P(None, ("sec", "ctx"), None),
        P(),
        P(None, "ctx"),
        P("ctx"),
        P("ctx", None),
        P(),
        P("sec", "ctx", None),
        P(),
        P("sec", "ctx", None),
        P(),
        P(),
        P(),
    )
    return jax.shard_map(
        local,
        mesh=mesh,
        in_specs=placed,
        out_specs=(P("sec", "ctx", None), P(None, ("sec", "ctx"), None)),
        check_vma=False,
    )
```

```python
import jax
import jax.numpy as jnp
from jax import lax
from jax.experimental import pallas as pl
from jax.experimental.pallas import tpu as pltpu
from jax.sharding import PartitionSpec as P

MESH = pl.DeviceIdType.MESH
F32 = jnp.float32
BF = jnp.bfloat16
SIDE = 4
SUBS = 4
HALF = 16
TILE = 512
RING = 4


def kernel(
    img_seq,
    img_off,
    img_cnt,
    patches_hbm,
    patch_gain_hbm,
    b_in_hbm,
    b_out_hbm,
    gain_hbm,
    w_in_hbm,
    w_out_hbm,
    text_hbm,
    up_hbm,
    normed_hbm,
    grad_hbm,
    w_in,
    w_own,
    w_sib,
    text,
    up,
    xn,
    xr,
    ys,
    yr,
    xbuf,
    acc,
    hid,
    hid_sib,
    sums,
    far_s,
    far_r,
    near_s,
    near_r,
    v_s,
    v,
    sus,
    nrm,
    stat,
    gs,
    gr,
    hs,
    hr,
    os_,
    own,
    patches,
    patch_gain_row,
    b_in_row,
    b_out_row,
    gain_row,
    patch_gain,
    b_in,
    b_out,
    gain,
    tab,
    loc,
    s_zs,
    r_zs,
    s_xy,
    r_xy,
    s_ag,
    r_ag,
    s_fw,
    r_fw,
    s_sib,
    r_sib,
    s_w,
    r_w,
    s_h,
    r_h,
    s_far,
    r_far,
    s_near,
    r_near,
    s_v,
    r_v,
    s_b1,
    r_b1,
    s_b2,
    r_b2,
    s_b3,
    r_b3,
):
    sec = lax.axis_index("sec")
    ctx = lax.axis_index("ctx")
    x, y = sec // SIDE, sec % SIDE
    z, k = ctx // 2, ctx % 2
    n_ctx = 2 * SIDE
    n_sec = SIDE * SIDE
    width = xn.shape[-1]
    tiles = far_s.shape[0]
    pieces = sus.shape[0]

    def at_ctx(c):
        return {"sec": sec, "ctx": c}

    def at_sec(s):
        return {"sec": s, "ctx": ctx}

    def plane_peer(d):
        return ((x + d // SIDE) % SIDE) * SIDE + (y + d % SIDE) % SIDE

    up_z = at_ctx(((z + 1) % SIDE) * 2 + k)
    down_z = at_ctx(((z + SIDE - 1) % SIDE) * 2 + k)
    sib = at_ctx(z * 2 + 1 - k)

    def remote(src, dst, ssem, rsem, device):
        return pltpu.make_async_remote_copy(
            src_ref=src,
            dst_ref=dst,
            send_sem=ssem,
            recv_sem=rsem,
            device_id=device,
            device_id_type=MESH,
        )

    cols = w_own.shape[1]
    small = [
        pltpu.make_async_copy(src, dst, loc.at[5 + SUBS + i])
        for i, (src, dst) in enumerate(
            (
                (patches_hbm, patches),
                (patch_gain_hbm, patch_gain_row),
                (b_in_hbm, b_in_row),
                (b_out_hbm, b_out_row),
                (gain_hbm, gain_row),
            )
        )
    ]
    load_up = pltpu.make_async_copy(up_hbm, up, loc.at[0])
    load_text = pltpu.make_async_copy(text_hbm, text, loc.at[1])
    load_in = pltpu.make_async_copy(w_in_hbm, w_in, loc.at[2])
    load_own = pltpu.make_async_copy(
        w_out_hbm.at[:, pl.ds(pl.multiple_of(k * cols, cols), cols)], w_own, loc.at[3]
    )

    barrier = pltpu.get_barrier_semaphore()

    def greet_ctx(d, carry):
        pl.semaphore_signal(
            barrier, inc=1, device_id=at_ctx((ctx + d) % n_ctx), device_id_type=MESH
        )
        return carry

    def greet_sec(d, carry):
        pl.semaphore_signal(barrier, inc=1, device_id=at_sec(plane_peer(d)), device_id_type=MESH)
        return carry

    lax.fori_loop(1, n_ctx, greet_ctx, 0)
    lax.fori_loop(1, n_sec, greet_sec, 0)
    for load in small:
        load.start()
    load_in.start()
    load_up.start()
    load_text.start()
    load_own.start()
    for load in small:
        load.wait()

    for row, line in (
        (patch_gain_row, patch_gain),
        (b_in_row, b_in),
        (b_out_row, b_out),
        (gain_row, gain),
    ):
        line[...] = row[...].reshape(line.shape)

    groups = patches.shape[2] // patch_gain.shape[1]
    group = patch_gain.shape[1]

    def norm_half(h):
        for i in range(2):
            for g in range(groups):
                f = patches[h * HALF : (h + 1) * HALF, i, pl.ds(g * group, group)].astype(F32)
                inv = lax.rsqrt(jnp.mean(f * f, axis=-1, keepdims=True) + 1e-06)
                f = (f * inv * patch_gain[...]).astype(BF)
                for b in range(group // width):
                    xn[h, g * (group // width) + b, i] = f[:, b * width : (b + 1) * width]

    def spread_half(h):
        def send_spread(d, carry):
            c = (ctx + d) % n_ctx
            remote(xn.at[h, c], xr[h].at[ctx], s_zs.at[h], r_zs.at[h], at_ctx(c)).start()
            return carry

        lax.fori_loop(1, n_ctx, send_spread, 0)
        xr[h][ctx] = xn[h, ctx]

    norm_half(0)
    pl.semaphore_wait(barrier, n_ctx + n_sec - 2)
    spread_half(0)
    norm_half(1)
    spread_half(1)
    send_w = remote(
        w_out_hbm.at[:, pl.ds(pl.multiple_of((1 - k) * cols, cols), cols)], w_sib, s_w, r_w, sib
    )

    def own_images(n, carry):
        tab[3, n] = img_seq[sec * n_sec + n]
        return carry

    def image_for(q, carry):
        found = jnp.int32(0)
        for n in range(n_sec):
            found = jnp.where(tab[3, n] == q, n, found)
        tab[0, q] = found
        return carry

    def image_from(g, carry):
        offset = jnp.int32(0)
        length = jnp.int32(0)
        for n in range(n_sec):
            hit = img_seq[g * n_sec + n] == sec
            offset = jnp.where(hit, img_off[g * n_sec + n], offset)
            length = jnp.where(hit, img_cnt[g * n_sec + n], length)
        tab[4, g] = offset
        tab[5, g] = length
        return carry

    def place_of(g, carry):
        before = jnp.int32(0)
        for n in range(n_sec):
            before = before + jnp.where(tab[4, n] < tab[4, g], 1, 0)
        tab[2, g] = before
        return carry

    def group_at(i, carry):
        found = jnp.int32(0)
        for n in range(n_sec):
            found = jnp.where(tab[2, n] == i, n, found)
        tab[1, i] = found
        return carry

    for fill in (own_images, image_for, image_from, place_of, group_at):
        lax.fori_loop(0, n_sec, fill, 0)

    for h in range(2):
        remote(
            xn.at[h, pl.ds(0, n_ctx - 1)], xr[h].at[pl.ds(0, n_ctx - 1)], s_zs.at[h], r_zs.at[h], sib
        ).wait_recv()

        def send_plane(d, carry, h=h):
            q = plane_peer(d)
            n = tab[0, q]
            ys[h, q] = xr[h][n // 2, n % 2]
            remote(ys.at[h, q], yr[h].at[sec], s_xy.at[h], r_xy.at[h], at_sec(q)).start()
            return carry

        lax.fori_loop(1, n_sec, send_plane, 0)
        n = tab[0, sec]
        yr[h][sec] = xr[h][n // 2, n % 2]
    send_w.start()

    rows = text.shape[0]
    first = [tab[4, tab[1, 2 * ctx + i]] - ctx * rows for i in range(2)]
    count = [tab[5, tab[1, 2 * ctx + i]] for i in range(2)]

    def placement(shape, slot_axis, row_axis):
        r = lax.broadcasted_iota(jnp.int32, shape, slot_axis)
        p = lax.broadcasted_iota(jnp.int32, shape, row_axis)
        slot = (r // (2 * HALF)) * HALF + r % HALF
        second = (r // HALF) % 2 == 1
        start = jnp.where(second, first[1], first[0])
        length = jnp.where(second, count[1], count[0])
        return jnp.where((slot < length) & (p == start + slot), 1.0, 0.0).astype(BF)

    def multiply(c, h, start=False):
        part = jnp.dot(
            xbuf[c, h],
            w_in[pl.ds(pl.multiple_of(c * width, width), width), :],
            preferred_element_type=F32,
        )
        acc[h] = part if start else acc[h] + part

    c_down = ((z + SIDE - 1) % SIDE) * 2 + k
    c_up = ((z + 1) % SIDE) * 2 + k
    c_far = ((z + 2) % SIDE) * 2 + k

    quarter = n_sec * HALF // 2

    def rows_of(c, u):
        return xbuf.at[c, u // 2, pl.ds((u % 2) * quarter, quarter)]

    def along(c, u, way, ssem, rsem):
        part = rows_of(c, u)
        return remote(part, part, ssem.at[way, u], rsem.at[way, u], up_z if way == 0 else down_z)

    def gather(c, u, way):
        return along(c, u, way, s_ag, r_ag)

    def forward(c, u, way):
        return along(c, u, way, s_fw, r_fw)

    def to_sib(c, u, rel):
        part = rows_of(c, u)
        return remote(part, part, s_sib.at[rel, u], r_sib.at[rel, u], sib)

    def other(c):
        return c + 1 - 2 * k

    ways = (0, 1, 1, 0)
    for h in range(2):
        remote(
            ys.at[h, pl.ds(0, n_sec - 1)], yr[h].at[pl.ds(0, n_sec - 1)], s_xy.at[h], r_xy.at[h], sib
        ).wait_recv()
        for u in (2 * h, 2 * h + 1):
            for i in range(n_sec // 2):
                xbuf[ctx, h, pl.ds((u % 2) * quarter + i * HALF, HALF), :] = yr[h][
                    tab[1, (u % 2) * (n_sec // 2) + i]
                ]
            for way in range(2):
                gather(ctx, u, way).start()
            to_sib(ctx, u, 0).start()
    load_in.wait()
    for h in range(2):
        multiply(ctx, h, start=True)

    load_up.wait()
    pick = placement((4 * HALF, rows), 0, 1)

    def gather_upstream(j, carry):
        at = pl.ds(pl.multiple_of(j * TILE, TILE), TILE)
        sus[j] = jnp.dot(pick, up[:, at], preferred_element_type=F32).astype(BF)
        return carry

    lax.fori_loop(0, pieces, gather_upstream, 0)
    load_text.wait()

    def norm_text(b, carry):
        at = pl.ds(pl.multiple_of(b * HALF, HALF), HALF)
        t = text[at, :].astype(F32)
        inv = lax.rsqrt(jnp.mean(t * t, axis=-1, keepdims=True) + 1e-06)
        nrm[at, :] = (t * inv * gain[...]).astype(BF)
        return carry

    lax.fori_loop(0, rows // HALF, norm_text, 0)
    for h in range(2):
        for u in (2 * h, 2 * h + 1):
            for way, c, rel in ((0, c_down, 3), (1, c_up, 1)):
                gather(c, u, way).wait_recv()
                if ways[u] == way:
                    forward(c, u, way).start()
                to_sib(c, u, rel).start()
        for u in (2 * h, 2 * h + 1):
            to_sib(other(ctx), u, 0).wait_recv()
        multiply(other(ctx), h)
        multiply(c_down, h)
        multiply(c_up, h)
        for c, rel in ((c_down, 3), (c_up, 1)):
            for u in (2 * h, 2 * h + 1):
                to_sib(other(c), u, rel).wait_recv()
            multiply(other(c), h)

    def activate(h):
        def body(c, carry):
            at = pl.ds(pl.multiple_of(c * 2 * HALF, 2 * HALF), 2 * HALF)
            pre = acc[h, at, :] + b_in[...]
            act = 0.5 * pre * (1.0 + lax.erf(pre * (0.5**0.5)))
            rel = (c // 2 + SIDE - z) % SIDE
            hid[h, rel, c % 2] = act.astype(BF)
            return carry

        lax.fori_loop(0, n_ctx, body, 0)

    def send_h(h):
        return remote(hid.at[h], hid_sib.at[h], s_h.at[h], r_h.at[h], sib)

    def product(left, h, right, t):
        at = pl.ds(pl.multiple_of(t * TILE, TILE), TILE)
        out = jnp.dot(
            left[h].reshape(-1, left.shape[-1]), right[:, at], preferred_element_type=F32
        )
        return out.reshape(SIDE, 2, 2 * HALF, TILE)

    for h in range(2):
        for u in (2 * h, 2 * h + 1):
            forward(c_far, u, ways[u]).wait_recv()
            to_sib(c_far, u, 2).start()
        multiply(c_far, h)
        for u in (2 * h, 2 * h + 1):
            to_sib(other(c_far), u, 2).wait_recv()
        multiply(other(c_far), h)
        activate(h)
        send_h(h).start()
        if h == 0:
            load_own.wait()
            send_w.wait_recv()
        sums[0, h] = product(hid, h, w_own, 0)

    def far(t, way):
        return remote(
            far_s.at[t, way],
            far_r.at[t, way],
            s_far.at[t, way],
            r_far.at[t, way],
            up_z if way == 0 else down_z,
        )

    def near(t, way):
        return remote(
            near_s.at[t, way],
            near_r.at[t, way],
            s_near.at[t, way],
            r_near.at[t, way],
            up_z if way == 0 else down_z,
        )

    def to_v(t):
        return remote(v_s.at[t], v.at[k * tiles + t], s_v.at[t], r_v.at[t], sib)

    def from_v(t):
        return remote(v_s.at[t], v.at[(1 - k) * tiles + t], s_v.at[t], r_v.at[t], sib)

    block = 4 * HALF

    def scatter_far(t):
        for way in range(2):
            far_s[t, way] = sums[t % RING, :, 2, way].astype(BF)
            far(t, way).start()

    def tally(j):
        val = v[j].astype(F32)
        scaled = sus[j].astype(F32) * gain[:, pl.ds(pl.multiple_of(j * TILE, TILE), TILE)]
        squares, inner = val * val, val * scaled
        for b in range(TILE // 128):
            stat[0] += squares[:, b * 128 : (b + 1) * 128]
            stat[1] += inner[:, b * 128 : (b + 1) * 128]

    stat[...] = jnp.zeros_like(stat)
    for h in range(2):
        send_h(h).wait_recv()
        sums[0, h] += product(hid_sib, h, w_sib, 0)
    scatter_far(0)

    def step(t, carry):
        @pl.when(t < tiles)
        def _():
            for h in range(2):
                sums[t % RING, h] = product(hid, h, w_own, t) + product(hid_sib, h, w_sib, t)
            scatter_far(t)

        @pl.when((t >= 2) & (t <= tiles + 1))
        def _():
            u = t - 2
            for way, rel in ((0, 1), (1, 3)):
                far(u, way).wait_recv()
                near_s[u, way, way] = (
                    sums[u % RING, :, rel, way] + far_r[u, way].astype(F32)
                ).astype(BF)
                near_s[u, way, 1 - way] = sums[u % RING, :, rel, 1 - way].astype(BF)
                near(u, way).start()

        @pl.when(t >= 3)
        def _():
            u = t - 3
            near(u, 0).wait_recv()
            near(u, 1).wait_recv()
            at = pl.ds(pl.multiple_of((k * tiles + u) * TILE, TILE), TILE)

            def whole(p):
                total = (
                    sums[u % RING, :, 0, p]
                    + near_r[u, 0, p].astype(F32)
                    + near_r[u, 1, p].astype(F32)
                )
                return (total.reshape(block, TILE) + b_out[:, at]).astype(BF)

            v_s[u] = whole(1 - k)
            to_v(u).start()
            v[k * tiles + u] = whole(k)
            tally(k * tiles + u)

        @pl.when(t >= 4)
        def _():
            from_v(t - 4).wait_recv()
            tally((1 - k) * tiles + t - 4)

        return carry

    lax.fori_loop(1, tiles + 3, step, 0)
    from_v(tiles - 1).wait_recv()
    tally((1 - k) * tiles + tiles - 1)

    model = pieces * TILE
    n_ctx_cols = model // n_ctx

    squares = jnp.sum(stat[0], axis=-1, keepdims=True)
    inner = jnp.sum(stat[1], axis=-1, keepdims=True)
    inv = lax.rsqrt(squares / model + 1e-06)
    pull = inv**3 * (inner / model)
    stat[0] = jnp.broadcast_to(inv, stat.shape[1:])
    stat[1] = jnp.broadcast_to(pull, stat.shape[1:])
    wide = gs.shape[-1]
    chunk = min(wide, TILE)

    def spread_back(sub, c):
        return remote(gs.at[sub, c], gr[sub].at[ctx], s_b1.at[sub], r_b1.at[sub], at_ctx(c))

    def gradient(sub, c, out):
        for b in range(wide // chunk):
            col = sub * wide + b * chunk
            j = c * (n_ctx_cols // TILE) + col // TILE
            at = pl.ds(pl.multiple_of(c * n_ctx_cols + col, chunk), chunk)
            inner = slice(col % TILE, col % TILE + chunk)
            scaled = sus[j, :, inner].astype(F32) * gain[:, at]
            val = stat[0, :, :1] * scaled - v[j, :, inner].astype(F32) * stat[1, :, :1]
            out[c, :, :, :, b * chunk : (b + 1) * chunk] = (
                val.astype(BF).reshape(2, 2, HALF, chunk)
            )

    for sub in range(SUBS):

        def send_back(d, carry, sub=sub):
            c = (ctx + d) % n_ctx
            gradient(sub, c, gs.at[sub])
            spread_back(sub, c).start()
            return carry

        lax.fori_loop(1, n_ctx, send_back, 0)
        gradient(sub, ctx, gr[sub])

    put = placement((rows, block), 1, 0)
    row = lax.broadcasted_iota(jnp.int32, (rows, 1), 0)
    covered = ((row >= first[0]) & (row < first[0] + count[0])) | (
        (row >= first[1]) & (row < first[1] + count[1])
    )

    def put_images(j, carry):
        at = pl.ds(pl.multiple_of(j * TILE, TILE), TILE)
        image = (v[j].astype(F32) * stat[0, :, :1] * gain[:, at]).astype(BF)
        placed = jnp.dot(put, image, preferred_element_type=F32)
        nrm[:, at] = jnp.where(covered, placed, nrm[:, at].astype(F32)).astype(BF)
        return carry

    def exchange_back(sub):
        spread_sizes = pl.ds(0, n_ctx - 1)
        remote(
            gs.at[sub, spread_sizes], gr[sub].at[spread_sizes], s_b1.at[sub], r_b1.at[sub], sib
        ).wait_recv()

        def send(d, carry):
            s = plane_peer(d)
            n = tab[2, s]
            for h in range(2):
                hs[sub, s, h] = gr[sub][n // 2, h, n % 2]
            remote(hs.at[sub, s], hr[sub].at[sec], s_b2.at[sub], r_b2.at[sub], at_sec(s)).start()
            return carry

        lax.fori_loop(1, n_sec, send, 0)
        n = tab[2, sec]
        for h in range(2):
            hr[sub][sec, h] = gr[sub][n // 2, h, n % 2]

    def block_of(c, sub):
        return pl.ds(pl.multiple_of(c * n_ctx_cols + sub * wide, wide), wide)

    def home(sub, c):
        return remote(
            os_.at[sub, c],
            grad_hbm.at[:, :, block_of(ctx, sub)],
            s_b3.at[sub],
            r_b3.at[sub],
            at_ctx(c),
        )

    def collect(sub, c, out):
        for i in range(2):
            for h in range(2):
                out[i, h * HALF : (h + 1) * HALF] = hr[sub][tab[3, 2 * c + i], h]

    def keep(sub):
        return pltpu.make_async_copy(
            own.at[sub], grad_hbm.at[:, :, block_of(ctx, sub)], loc.at[5 + sub]
        )

    def exchange_home(sub):
        plane_sizes = pl.ds(0, n_sec - 1)
        remote(
            hs.at[sub, plane_sizes], hr[sub].at[plane_sizes], s_b2.at[sub], r_b2.at[sub], sib
        ).wait_recv()

        def send(d, carry):
            c = (ctx + d) % n_ctx
            collect(sub, c, os_.at[sub, c])
            home(sub, c).start()
            return carry

        lax.fori_loop(1, n_ctx, send, 0)
        collect(sub, ctx, own.at[sub])
        keep(sub).start()

    for sub in range(SUBS):
        exchange_back(sub)
        share = pieces // SUBS
        lax.fori_loop(sub * share, (sub + 1) * share, put_images, 0)
    store_normed = pltpu.make_async_copy(nrm, normed_hbm, loc.at[4])
    store_normed.start()
    for sub in range(SUBS):
        exchange_home(sub)
    last = pl.ds(0, n_ctx - 1)

    def all_home(sub, part):
        return remote(part, part, s_b3.at[sub], r_b3.at[sub], sib)

    for sub in range(SUBS):
        all_home(sub, grad_hbm.at[:, :, pl.ds(0, (n_ctx - 1) * wide)]).wait_recv()

    for h in range(2):
        remote(xn.at[h, last], xr[h].at[last], s_zs.at[h], r_zs.at[h], sib).wait_send()
        plane = pl.ds(0, n_sec - 1)
        remote(ys.at[h, plane], yr[h].at[plane], s_xy.at[h], r_xy.at[h], sib).wait_send()
        send_h(h).wait_send()
    for u in range(4):
        for way in range(2):
            gather(ctx, u, way).wait_send()
        forward(ctx, u, ways[u]).wait_send()
        for rel in range(SIDE):
            to_sib(ctx, u, rel).wait_send()
    send_w.wait_send()

    def drain(t, carry):
        for way in range(2):
            far(t, way).wait_send()
            near(t, way).wait_send()
        to_v(t).wait_send()
        return carry

    lax.fori_loop(0, tiles, drain, 0)
    for sub in range(SUBS):
        plane = pl.ds(0, n_sec - 1)
        remote(gs.at[sub, last], gr[sub].at[last], s_b1.at[sub], r_b1.at[sub], sib).wait_send()
        remote(hs.at[sub, plane], hr[sub].at[plane], s_b2.at[sub], r_b2.at[sub], sib).wait_send()

        all_home(sub, os_.at[sub, last]).wait_send()
        keep(sub).wait()
    store_normed.wait()


def local(
    patches,
    patch_gain,
    w_merge_in,
    b_merge_in,
    w_merge_out,
    b_merge_out,
    text_embed,
    norm_gain,
    upstream,
    img_seq,
    img_off,
    img_cnt,
):
    slot_count, own_images, hidden_width = patches.shape
    n_sec = lax.axis_size("sec")
    n_ctx = lax.axis_size("ctx")
    seq_rows, model = text_embed.shape[1:]
    width = hidden_width // n_ctx
    hidden = w_merge_in.shape[1]
    cols = model // 2
    tiles = cols // TILE
    pieces = model // TILE
    wide = model // n_ctx // SUBS
    block = 4 * HALF
    smem = pl.BlockSpec(memory_space=pltpu.SMEM)
    vmem = pl.BlockSpec(memory_space=pltpu.VMEM)
    hbm = pl.BlockSpec(memory_space=pl.ANY)
    dma = pltpu.SemaphoreType.DMA
    normed, grads = pl.pallas_call(
        kernel,
        out_shape=(
            jax.ShapeDtypeStruct((seq_rows, model), BF),
            jax.ShapeDtypeStruct((own_images, slot_count, model), BF),
        ),
        in_specs=[smem] * 3 + [hbm] * 9,
        out_specs=(hbm, hbm),
        scratch_shapes=[
            pltpu.VMEM((hidden_width, hidden), BF),
            pltpu.VMEM((hidden, cols), BF),
            pltpu.VMEM((hidden, cols), BF),
            pltpu.VMEM((seq_rows, model), BF),
            pltpu.VMEM((seq_rows, model), BF),
            pltpu.VMEM((2, n_ctx, 2, HALF, width), BF),
            [pltpu.VMEM((n_ctx, 2, HALF, width), BF)] * 2,
            pltpu.VMEM((2, n_sec, HALF, width), BF),
            [pltpu.VMEM((n_sec, HALF, width), BF)] * 2,
            pltpu.VMEM((n_ctx, 2, n_sec * HALF, width), BF),
            pltpu.VMEM((2, n_sec * HALF, hidden), F32),
            pltpu.VMEM((2, SIDE, 2, 2 * HALF, hidden), BF),
            pltpu.VMEM((2, SIDE, 2, 2 * HALF, hidden), BF),
            pltpu.VMEM((RING, 2, SIDE, 2, 2 * HALF, TILE), F32),
            pltpu.VMEM((tiles, 2, 2, 2 * HALF, TILE), BF),
            pltpu.VMEM((tiles, 2, 2, 2 * HALF, TILE), BF),
            pltpu.VMEM((tiles, 2, 2, 2, 2 * HALF, TILE), BF),
            pltpu.VMEM((tiles, 2, 2, 2, 2 * HALF, TILE), BF),
            pltpu.VMEM((tiles, block, TILE), BF),
            pltpu.VMEM((pieces, block, TILE), BF),
            pltpu.VMEM((pieces, block, TILE), BF),
            pltpu.VMEM((seq_rows, model), BF),
            pltpu.VMEM((2, block, 128), F32),
            pltpu.VMEM((SUBS, n_ctx, 2, 2, HALF, wide), BF),
            [pltpu.VMEM((n_ctx, 2, 2, HALF, wide), BF)] * SUBS,
            pltpu.VMEM((SUBS, n_sec, 2, HALF, wide), BF),
            [pltpu.VMEM((n_sec, 2, HALF, wide), BF)] * SUBS,
            pltpu.VMEM((SUBS, n_ctx, own_images, slot_count, wide), BF),
            pltpu.VMEM((SUBS, own_images, slot_count, wide), BF),
            pltpu.VMEM(patches.shape, BF),
            pltpu.VMEM(patch_gain.shape, F32),
            pltpu.VMEM((hidden,), F32),
            pltpu.VMEM((model,), F32),
            pltpu.VMEM((model,), F32),
            pltpu.VMEM((1, patch_gain.shape[0]), F32),
            pltpu.VMEM((1, hidden), F32),
            pltpu.VMEM((1, model), F32),
            pltpu.VMEM((1, model), F32),
            pltpu.SMEM((6, n_sec), jnp.int32),
            dma((10 + SUBS,)),
            dma((2,)),
            dma((2,)),
            dma((2,)),
            dma((2,)),
            dma((2, 4)),
            dma((2, 4)),
            dma((2, 4)),
            dma((2, 4)),
            dma((SIDE, 4)),
            dma((SIDE, 4)),
            dma,
            dma,
            dma((2,)),
            dma((2,)),
            dma((tiles, 2)),
            dma((tiles, 2)),
            dma((tiles, 2)),
            dma((tiles, 2)),
            dma((tiles,)),
            dma((tiles,)),
            dma((SUBS,)),
            dma((SUBS,)),
            dma((SUBS,)),
            dma((SUBS,)),
            dma((SUBS,)),
            dma((SUBS,)),
        ],
        compiler_params=pltpu.CompilerParams(
            collective_id=0, has_side_effects=True, vmem_limit_bytes=63 << 20
        ),
        name="merger",
    )(
        img_seq,
        img_off,
        img_cnt,
        patches,
        patch_gain,
        b_merge_in,
        b_merge_out,
        norm_gain,
        w_merge_in,
        w_merge_out,
        text_embed[0],
        upstream[0],
    )
    image_grad = grads.transpose(1, 0, 2)
    return (normed[None], image_grad)


def solution(mesh):
    placed = (
        P(None, ("sec", "ctx"), None),
        P(),
        P(None, "ctx"),
        P("ctx"),
        P("ctx", None),
        P(),
        P("sec", "ctx", None),
        P(),
        P("sec", "ctx", None),
        P(),
        P(),
        P(),
    )
    return jax.shard_map(
        local,
        mesh=mesh,
        in_specs=placed,
        out_specs=(P("sec", "ctx", None), P(None, ("sec", "ctx"), None)),
        check_vma=False,
    )
```

```python
import jax
import jax.numpy as jnp
from jax import lax
from jax.experimental import pallas as pl
from jax.experimental.pallas import tpu as pltpu
from jax.sharding import PartitionSpec as P

MESH = pl.DeviceIdType.MESH
F32 = jnp.float32
BF = jnp.bfloat16
SIDE = 4
PIECES = 4
SUBS = 8
HALF = 16
TILE = 512
AHEAD = 4
RING = AHEAD + 2
LAGS = (4, 4)
EARLY = 2
PART_LAG = 3


def kernel(
    img_seq,
    img_off,
    img_cnt,
    patches_hbm,
    patch_gain_hbm,
    b_in_hbm,
    b_out_hbm,
    gain_hbm,
    w_in_hbm,
    w_out_hbm,
    text_hbm,
    up_hbm,
    normed_hbm,
    grad_hbm,
    w_in,
    w_own,
    w_sib,
    text,
    up,
    xn,
    xr,
    ys,
    yr,
    xbuf,
    acc,
    hid,
    hid_sib,
    sums,
    far_s,
    far_r,
    near_s,
    near_r,
    v_s,
    v,
    sus,
    nrm,
    stat,
    gs,
    gr,
    hs,
    hr,
    os_,
    own,
    patches,
    patch_gain_row,
    b_in_row,
    b_out_row,
    gain_row,
    patch_gain,
    b_in,
    b_out,
    gain,
    tab,
    loc,
    s_zs,
    r_zs,
    s_xy,
    r_xy,
    s_ag,
    r_ag,
    s_fw,
    r_fw,
    s_sib,
    r_sib,
    s_w,
    r_w,
    s_h,
    r_h,
    s_far,
    r_far,
    s_near,
    r_near,
    s_v,
    r_v,
    s_b1,
    r_b1,
    s_b2,
    r_b2,
    s_b3,
    r_b3,
):
    sec = lax.axis_index("sec")
    ctx = lax.axis_index("ctx")
    x, y = sec // SIDE, sec % SIDE
    z, k = ctx // 2, ctx % 2
    n_ctx = 2 * SIDE
    n_sec = SIDE * SIDE
    widths = [part.shape[-1] for part in xn]
    starts = [0, widths[0]]
    width = sum(widths)
    parts = 2 * len(widths)
    tiles = far_s.shape[0]
    pieces = sus.shape[0]

    def at_ctx(c):
        return {"sec": sec, "ctx": c}

    def at_sec(s):
        return {"sec": s, "ctx": ctx}

    def plane_peer(d):
        return ((x + d // SIDE) % SIDE) * SIDE + (y + d % SIDE) % SIDE

    up_z = at_ctx(((z + 1) % SIDE) * 2 + k)
    down_z = at_ctx(((z + SIDE - 1) % SIDE) * 2 + k)
    sib = at_ctx(z * 2 + 1 - k)

    def remote(src, dst, ssem, rsem, device):
        return pltpu.make_async_remote_copy(
            src_ref=src,
            dst_ref=dst,
            send_sem=ssem,
            recv_sem=rsem,
            device_id=device,
            device_id_type=MESH,
        )

    cols = w_own.shape[1]
    small = [
        pltpu.make_async_copy(src, dst, loc.at[5 + SUBS + i])
        for i, (src, dst) in enumerate(
            (
                (patches_hbm, patches),
                (patch_gain_hbm, patch_gain_row),
                (b_in_hbm, b_in_row),
                (b_out_hbm, b_out_row),
                (gain_hbm, gain_row),
            )
        )
    ]
    load_up = pltpu.make_async_copy(up_hbm, up, loc.at[0])
    load_text = pltpu.make_async_copy(text_hbm, text, loc.at[1])
    load_in = pltpu.make_async_copy(w_in_hbm, w_in, loc.at[2])
    load_own = pltpu.make_async_copy(
        w_out_hbm.at[:, pl.ds(pl.multiple_of(k * cols, cols), cols)], w_own, loc.at[3]
    )

    barrier = pltpu.get_barrier_semaphore()

    def greet_ctx(d, carry):
        pl.semaphore_signal(
            barrier, inc=1, device_id=at_ctx((ctx + d) % n_ctx), device_id_type=MESH
        )
        return carry

    def greet_sec(d, carry):
        pl.semaphore_signal(barrier, inc=1, device_id=at_sec(plane_peer(d)), device_id_type=MESH)
        return carry

    lax.fori_loop(1, n_ctx, greet_ctx, 0)
    lax.fori_loop(1, n_sec, greet_sec, 0)
    for load in small:
        load.start()
    load_in.start()
    load_up.start()
    load_text.start()
    load_own.start()
    for load in small:
        load.wait()

    for row, line in (
        (patch_gain_row, patch_gain),
        (b_in_row, b_in),
        (b_out_row, b_out),
        (gain_row, gain),
    ):
        line[...] = row[...].reshape(line.shape)

    groups = patches.shape[2] // patch_gain.shape[1]
    group = patch_gain.shape[1]

    def norm_half(h):
        for i in range(2):
            for g in range(groups):
                f = patches[h * HALF : (h + 1) * HALF, i, pl.ds(g * group, group)].astype(F32)
                inv = lax.rsqrt(jnp.mean(f * f, axis=-1, keepdims=True) + 1e-06)
                f = (f * inv * patch_gain[...]).astype(BF)
                for b in range(group // width):
                    for part, start in zip(xn, starts):
                        at = b * width + start
                        part[h, g * (group // width) + b, i] = f[:, at : at + part.shape[-1]]

    def spread(u):
        h, mine = u // 2, xn[u % 2]

        def send_spread(d, carry):
            c = (ctx + d) % n_ctx
            remote(mine.at[h, c], xr[u].at[ctx], s_zs.at[u], r_zs.at[u], at_ctx(c)).start()
            return carry

        lax.fori_loop(1, n_ctx, send_spread, 0)
        xr[u][ctx] = mine[h, ctx]

    norm_half(0)
    pl.semaphore_wait(barrier, n_ctx + n_sec - 2)
    spread(0)
    spread(1)
    norm_half(1)
    spread(2)
    spread(3)
    send_w = remote(
        w_out_hbm.at[:, pl.ds(pl.multiple_of((1 - k) * cols, cols), cols)], w_sib, s_w, r_w, sib
    )

    def own_images(n, carry):
        tab[3, n] = img_seq[sec * n_sec + n]
        return carry

    def image_for(q, carry):
        found = jnp.int32(0)
        for n in range(n_sec):
            found = jnp.where(tab[3, n] == q, n, found)
        tab[0, q] = found
        return carry

    def image_from(g, carry):
        offset = jnp.int32(0)
        length = jnp.int32(0)
        for n in range(n_sec):
            hit = img_seq[g * n_sec + n] == sec
            offset = jnp.where(hit, img_off[g * n_sec + n], offset)
            length = jnp.where(hit, img_cnt[g * n_sec + n], length)
        tab[4, g] = offset
        tab[5, g] = length
        return carry

    def place_of(g, carry):
        before = jnp.int32(0)
        for n in range(n_sec):
            before = before + jnp.where(tab[4, n] < tab[4, g], 1, 0)
        tab[2, g] = before
        return carry

    def group_at(i, carry):
        found = jnp.int32(0)
        for n in range(n_sec):
            found = jnp.where(tab[2, n] == i, n, found)
        tab[1, i] = found
        return carry

    for fill in (own_images, image_for, image_from, place_of, group_at):
        lax.fori_loop(0, n_sec, fill, 0)

    def all_spread(u):
        most = pl.ds(0, n_ctx - 1)
        return remote(xn[u % 2].at[u // 2, most], xr[u].at[most], s_zs.at[u], r_zs.at[u], sib)

    def all_plane(u):
        most = pl.ds(0, n_sec - 1)
        return remote(ys[u].at[most], yr[u].at[most], s_xy.at[u], r_xy.at[u], sib)

    def to_plane(u):
        all_spread(u).wait_recv()

        def send_plane(d, carry):
            q = plane_peer(d)
            n = tab[0, q]
            ys[u][q] = xr[u][n // 2, n % 2]
            remote(ys[u].at[q], yr[u].at[sec], s_xy.at[u], r_xy.at[u], at_sec(q)).start()
            return carry

        lax.fori_loop(1, n_sec, send_plane, 0)
        n = tab[0, sec]
        yr[u][sec] = xr[u][n // 2, n % 2]

    rows = text.shape[0]
    first = [tab[4, tab[1, 2 * ctx + i]] - ctx * rows for i in range(2)]
    count = [tab[5, tab[1, 2 * ctx + i]] for i in range(2)]

    def placement(shape, slot_axis, row_axis):
        r = lax.broadcasted_iota(jnp.int32, shape, slot_axis)
        p = lax.broadcasted_iota(jnp.int32, shape, row_axis)
        slot = (r // (2 * HALF)) * HALF + r % HALF
        second = (r // HALF) % 2 == 1
        start = jnp.where(second, first[1], first[0])
        length = jnp.where(second, count[1], count[0])
        return jnp.where((slot < length) & (p == start + slot), 1.0, 0.0).astype(BF)

    def multiply(c, h, start=False):
        total = None if start else acc[h]
        for part, at in zip(xbuf, starts):
            rows_at = pl.ds(pl.multiple_of(c * width + at, 128), part.shape[-1])
            more = jnp.dot(part[c, h], w_in[rows_at, :], preferred_element_type=F32)
            total = more if total is None else total + more
        acc[h] = total

    c_down = ((z + SIDE - 1) % SIDE) * 2 + k
    c_up = ((z + 1) % SIDE) * 2 + k
    c_far = ((z + 2) % SIDE) * 2 + k

    def rows_of(c, u):
        return xbuf[u % 2].at[c, u // 2]

    def along(c, u, way, ssem, rsem):
        part = rows_of(c, u)
        return remote(part, part, ssem.at[way, u], rsem.at[way, u], up_z if way == 0 else down_z)

    def gather(c, u, way):
        return along(c, u, way, s_ag, r_ag)

    def forward(c, u, way):
        return along(c, u, way, s_fw, r_fw)

    def to_sib(c, u, rel):
        part = rows_of(c, u)
        return remote(part, part, s_sib.at[rel, u], r_sib.at[rel, u], sib)

    def other(c):
        return c + 1 - 2 * k

    ways = (0, 1, 1, 0)
    def to_ring(u):
        all_plane(u).wait_recv()
        for i in range(n_sec):
            xbuf[u % 2][ctx, u // 2, pl.ds(i * HALF, HALF), :] = yr[u][tab[1, i]]
        for way in range(2):
            gather(ctx, u, way).start()
        to_sib(ctx, u, 0).start()

    for n in range(parts + PART_LAG):
        if n < parts:
            to_plane(n)
        if n >= PART_LAG:
            to_ring(n - PART_LAG)
    send_w.start()
    load_in.wait()
    for h in range(2):
        multiply(ctx, h, start=True)

    load_up.wait()
    pick = placement((4 * HALF, rows), 0, 1)

    def gather_upstream(j, carry):
        at = pl.ds(pl.multiple_of(j * TILE, TILE), TILE)
        sus[j] = jnp.dot(pick, up[:, at], preferred_element_type=F32).astype(BF)
        return carry

    lax.fori_loop(0, pieces, gather_upstream, 0)
    load_text.wait()

    def norm_text(b, carry):
        at = pl.ds(pl.multiple_of(b * HALF, HALF), HALF)
        t = text[at, :].astype(F32)
        inv = lax.rsqrt(jnp.mean(t * t, axis=-1, keepdims=True) + 1e-06)
        nrm[at, :] = (t * inv * gain[...]).astype(BF)
        return carry

    lax.fori_loop(0, rows // HALF, norm_text, 0)
    for h in range(2):
        for u in (2 * h, 2 * h + 1):
            for way, c, rel in ((0, c_down, 3), (1, c_up, 1)):
                gather(c, u, way).wait_recv()
                if ways[u] == way:
                    forward(c, u, way).start()
                to_sib(c, u, rel).start()
        for u in (2 * h, 2 * h + 1):
            to_sib(other(ctx), u, 0).wait_recv()
        multiply(other(ctx), h)
        multiply(c_down, h)
        multiply(c_up, h)
        for c, rel in ((c_down, 3), (c_up, 1)):
            for u in (2 * h, 2 * h + 1):
                to_sib(other(c), u, rel).wait_recv()
            multiply(other(c), h)

    def activate(h):
        def body(c, carry):
            at = pl.ds(pl.multiple_of(c * 2 * HALF, 2 * HALF), 2 * HALF)
            pre = acc[h, at, :] + b_in[...]
            act = 0.5 * pre * (1.0 + lax.erf(pre * (0.5**0.5)))
            rel = (c // 2 + SIDE - z) % SIDE
            hid[h, rel, c % 2] = act.astype(BF)
            return carry

        lax.fori_loop(0, n_ctx, body, 0)

    def send_h(h):
        return remote(hid.at[h], hid_sib.at[h], s_h.at[h], r_h.at[h], sib)

    def product(left, h, right, t):
        at = pl.ds(pl.multiple_of(t * TILE, TILE), TILE)
        out = jnp.dot(
            left[h].reshape(-1, left.shape[-1]), right[:, at], preferred_element_type=F32
        )
        return out.reshape(SIDE, 2, 2 * HALF, TILE)

    def far_half(t, way, h):
        return remote(
            far_s.at[t, way, h],
            far_r.at[t, way, h],
            s_far.at[t, way],
            r_far.at[t, way],
            up_z if way == 0 else down_z,
        )

    def early(h):
        send_h(h).wait_recv()
        for t in range(EARLY):
            sums[t, h] += product(hid_sib, h, w_sib, t)
            for way in range(2):
                far_s[t, way, h] = sums[t, h, 2, way].astype(BF)
                far_half(t, way, h).start()

    for h in range(2):
        for u in (2 * h, 2 * h + 1):
            forward(c_far, u, ways[u]).wait_recv()
            to_sib(c_far, u, 2).start()
        multiply(c_far, h)
        if h == 1:
            early(0)
        for u in (2 * h, 2 * h + 1):
            to_sib(other(c_far), u, 2).wait_recv()
        multiply(other(c_far), h)
        activate(h)
        send_h(h).start()
        if h == 0:
            load_own.wait()
            send_w.wait_recv()
        for t in range(EARLY):
            sums[t, h] = product(hid, h, w_own, t)
    early(1)

    def far(t, way):
        return remote(
            far_s.at[t, way],
            far_r.at[t, way],
            s_far.at[t, way],
            r_far.at[t, way],
            up_z if way == 0 else down_z,
        )

    def near(t, way):
        return remote(
            near_s.at[t, way],
            near_r.at[t, way],
            s_near.at[t, way],
            r_near.at[t, way],
            up_z if way == 0 else down_z,
        )

    def to_v(t):
        return remote(v_s.at[t], v.at[k * tiles + t], s_v.at[t], r_v.at[t], sib)

    def from_v(t):
        return remote(v_s.at[t], v.at[(1 - k) * tiles + t], s_v.at[t], r_v.at[t], sib)

    block = 4 * HALF

    def scatter_far(t):
        for way in range(2):
            far_s[t, way] = sums[t % RING, :, 2, way].astype(BF)
            far(t, way).start()

    def tally(j):
        val = v[j].astype(F32)
        scaled = sus[j].astype(F32) * gain[:, pl.ds(pl.multiple_of(j * TILE, TILE), TILE)]
        squares, inner = val * val, val * scaled
        for b in range(TILE // 128):
            stat[0] += squares[:, b * 128 : (b + 1) * 128]
            stat[1] += inner[:, b * 128 : (b + 1) * 128]

    stat[...] = jnp.zeros_like(stat)

    def step(t, carry):
        @pl.when(t < tiles)
        def _():
            for h in range(2):
                sums[t % RING, h] = product(hid, h, w_own, t) + product(hid_sib, h, w_sib, t)
            scatter_far(t)

        @pl.when((t >= AHEAD) & (t < tiles + AHEAD))
        def _():
            u = t - AHEAD
            for way, rel in ((0, 1), (1, 3)):
                far(u, way).wait_recv()
                near_s[u, way, way] = (
                    sums[u % RING, :, rel, way] + far_r[u, way].astype(F32)
                ).astype(BF)
                near_s[u, way, 1 - way] = sums[u % RING, :, rel, 1 - way].astype(BF)
                near(u, way).start()

        @pl.when((t > AHEAD) & (t <= tiles + AHEAD))
        def _():
            u = t - AHEAD - 1
            near(u, 0).wait_recv()
            near(u, 1).wait_recv()
            at = pl.ds(pl.multiple_of((k * tiles + u) * TILE, TILE), TILE)

            def whole(p):
                total = (
                    sums[u % RING, :, 0, p]
                    + near_r[u, 0, p].astype(F32)
                    + near_r[u, 1, p].astype(F32)
                )
                return (total.reshape(block, TILE) + b_out[:, at]).astype(BF)

            v_s[u] = whole(1 - k)
            to_v(u).start()
            v[k * tiles + u] = whole(k)
            tally(k * tiles + u)

        @pl.when(t > AHEAD + 1)
        def _():
            u = t - AHEAD - 2
            from_v(u).wait_recv()
            tally((1 - k) * tiles + u)

        return carry

    lax.fori_loop(EARLY, tiles + AHEAD + 1, step, 0)
    from_v(tiles - 1).wait_recv()
    tally((1 - k) * tiles + tiles - 1)

    model = pieces * TILE
    n_ctx_cols = model // n_ctx

    squares = jnp.sum(stat[0], axis=-1, keepdims=True)
    inner = jnp.sum(stat[1], axis=-1, keepdims=True)
    inv = lax.rsqrt(squares / model + 1e-06)
    pull = inv**3 * (inner / model)
    stat[0] = jnp.broadcast_to(inv, stat.shape[1:])
    stat[1] = jnp.broadcast_to(pull, stat.shape[1:])
    wide = gs.shape[-1]
    chunk = min(wide, TILE)

    def spread_back(sub, c):
        return remote(gs.at[sub, c], gr[sub].at[ctx], s_b1.at[sub], r_b1.at[sub], at_ctx(c))

    def gradient(sub, c, out):
        for b in range(wide // chunk):
            col = sub * wide + b * chunk
            j = c * (n_ctx_cols // TILE) + col // TILE
            at = pl.ds(pl.multiple_of(c * n_ctx_cols + col, chunk), chunk)
            inner = slice(col % TILE, col % TILE + chunk)
            scaled = sus[j, :, inner].astype(F32) * gain[:, at]
            val = stat[0, :, :1] * scaled - v[j, :, inner].astype(F32) * stat[1, :, :1]
            out[c, :, :, :, b * chunk : (b + 1) * chunk] = (
                val.astype(BF).reshape(2, 2, HALF, chunk)
            )

    def send_gradient(sub):
        def send_back(d, carry):
            c = (ctx + d) % n_ctx
            gradient(sub, c, gs.at[sub])
            spread_back(sub, c).start()
            return carry

        lax.fori_loop(1, n_ctx, send_back, 0)
        gradient(sub, ctx, gr[sub])

    put = placement((rows, block), 1, 0)
    row = lax.broadcasted_iota(jnp.int32, (rows, 1), 0)
    covered = ((row >= first[0]) & (row < first[0] + count[0])) | (
        (row >= first[1]) & (row < first[1] + count[1])
    )

    def put_images(j, carry):
        at = pl.ds(pl.multiple_of(j * TILE, TILE), TILE)
        image = (v[j].astype(F32) * stat[0, :, :1] * gain[:, at]).astype(BF)
        placed = jnp.dot(put, image, preferred_element_type=F32)
        nrm[:, at] = jnp.where(covered, placed, nrm[:, at].astype(F32)).astype(BF)
        return carry

    def exchange_back(sub):
        spread_sizes = pl.ds(0, n_ctx - 1)
        remote(
            gs.at[sub, spread_sizes], gr[sub].at[spread_sizes], s_b1.at[sub], r_b1.at[sub], sib
        ).wait_recv()

        def send(d, carry):
            s = plane_peer(d)
            n = tab[2, s]
            for h in range(2):
                hs[sub, s, h] = gr[sub][n // 2, h, n % 2]
            remote(hs.at[sub, s], hr[sub].at[sec], s_b2.at[sub], r_b2.at[sub], at_sec(s)).start()
            return carry

        lax.fori_loop(1, n_sec, send, 0)
        n = tab[2, sec]
        for h in range(2):
            hr[sub][sec, h] = gr[sub][n // 2, h, n % 2]

    def block_of(c, sub):
        return pl.ds(pl.multiple_of(c * n_ctx_cols + sub * wide, wide), wide)

    def home(sub, c):
        return remote(
            os_.at[sub, c],
            grad_hbm.at[:, :, block_of(ctx, sub)],
            s_b3.at[sub],
            r_b3.at[sub],
            at_ctx(c),
        )

    def collect(sub, c, out):
        for h in range(2):
            pair = [hr[sub][tab[3, 2 * c + i], h] for i in range(2)]
            out[h * HALF : (h + 1) * HALF] = jnp.stack(pair, axis=1)

    def keep(sub):
        return pltpu.make_async_copy(
            own.at[sub], grad_hbm.at[:, :, block_of(ctx, sub)], loc.at[5 + sub]
        )

    def exchange_home(sub):
        plane_sizes = pl.ds(0, n_sec - 1)
        remote(
            hs.at[sub, plane_sizes], hr[sub].at[plane_sizes], s_b2.at[sub], r_b2.at[sub], sib
        ).wait_recv()

        def send(d, carry):
            c = (ctx + d) % n_ctx
            collect(sub, c, os_.at[sub, c])
            home(sub, c).start()
            return carry

        lax.fori_loop(1, n_ctx, send, 0)
        collect(sub, ctx, own.at[sub])
        keep(sub).start()

    second, third = LAGS[0], sum(LAGS)
    done = 0
    for n in range(SUBS + third):
        if n < SUBS:
            send_gradient(n)
        if second <= n < SUBS + second:
            exchange_back(n - second)
        if n >= third:
            exchange_home(n - third)
        if n >= SUBS + second:
            upto = pieces * (n - SUBS - second + 1) // LAGS[1]
            lax.fori_loop(done, upto, put_images, 0)
            done = upto
    store_normed = pltpu.make_async_copy(nrm, normed_hbm, loc.at[4])
    store_normed.start()
    last = pl.ds(0, n_ctx - 1)

    def all_home(sub, part):
        return remote(part, part, s_b3.at[sub], r_b3.at[sub], sib)

    for sub in range(SUBS):
        all_home(sub, grad_hbm.at[:, :, pl.ds(0, (n_ctx - 1) * wide)]).wait_recv()

    for h in range(2):
        send_h(h).wait_send()
    for u in range(parts):
        all_spread(u).wait_send()
        all_plane(u).wait_send()
        for way in range(2):
            gather(ctx, u, way).wait_send()
        forward(ctx, u, ways[u]).wait_send()
        for rel in range(SIDE):
            to_sib(ctx, u, rel).wait_send()
    send_w.wait_send()

    def drain(t, carry):
        for way in range(2):
            far(t, way).wait_send()
            near(t, way).wait_send()
        to_v(t).wait_send()
        return carry

    lax.fori_loop(0, tiles, drain, 0)
    for sub in range(SUBS):
        plane = pl.ds(0, n_sec - 1)
        remote(gs.at[sub, last], gr[sub].at[last], s_b1.at[sub], r_b1.at[sub], sib).wait_send()
        remote(hs.at[sub, plane], hr[sub].at[plane], s_b2.at[sub], r_b2.at[sub], sib).wait_send()

        all_home(sub, os_.at[sub, last]).wait_send()
        keep(sub).wait()
    store_normed.wait()


def finish(normed_in, grads_in, normed_out, grads_out, normed, grads, sems):
    rows = normed.shape[0] // PIECES
    slots = grads.shape[0] // PIECES
    pairs = []
    for n in range(PIECES):
        at = pl.ds(n * rows, rows)
        pairs.append((normed_in.at[at], normed.at[at], normed_out.at[at]))
        at = pl.ds(n * slots, slots)
        pairs.append((grads_in.at[at], grads.at[at], grads_out.at[at]))
    loads = [
        pltpu.make_async_copy(a, b, sems.at[0, i]) for i, (a, b, _) in enumerate(pairs)
    ]
    stores = [
        pltpu.make_async_copy(b, c, sems.at[1, i]) for i, (_, b, c) in enumerate(pairs)
    ]
    for load in loads:
        load.start()
    for load, store in zip(loads, stores):
        load.wait()
        store.start()
    for store in stores:
        store.wait()


def hand_over(normed, grads):
    hbm = pl.BlockSpec(memory_space=pl.ANY)
    return pl.pallas_call(
        finish,
        out_shape=[jax.ShapeDtypeStruct(a.shape, a.dtype) for a in (normed, grads)],
        in_specs=[hbm] * 2,
        out_specs=[hbm] * 2,
        scratch_shapes=[
            pltpu.VMEM(normed.shape, normed.dtype),
            pltpu.VMEM(grads.shape, grads.dtype),
            pltpu.SemaphoreType.DMA((2, 2 * PIECES)),
        ],
        compiler_params=pltpu.CompilerParams(vmem_limit_bytes=63 << 20),
        name="finish",
    )(normed, grads)


def local(
    patches,
    patch_gain,
    w_merge_in,
    b_merge_in,
    w_merge_out,
    b_merge_out,
    text_embed,
    norm_gain,
    upstream,
    img_seq,
    img_off,
    img_cnt,
):
    slot_count, own_images, hidden_width = patches.shape
    n_sec = lax.axis_size("sec")
    n_ctx = lax.axis_size("ctx")
    seq_rows, model = text_embed.shape[1:]
    width = hidden_width // n_ctx
    widths = [(width // 128 + 1) // 2 * 128]
    widths.append(width - widths[0])
    hidden = w_merge_in.shape[1]
    cols = model // 2
    tiles = cols // TILE
    pieces = model // TILE
    wide = model // n_ctx // SUBS
    block = 4 * HALF
    smem = pl.BlockSpec(memory_space=pltpu.SMEM)
    vmem = pl.BlockSpec(memory_space=pltpu.VMEM)
    hbm = pl.BlockSpec(memory_space=pl.ANY)
    dma = pltpu.SemaphoreType.DMA
    normed, grads = pl.pallas_call(
        kernel,
        out_shape=(
            jax.ShapeDtypeStruct((seq_rows, model), BF),
            jax.ShapeDtypeStruct((slot_count, own_images, model), BF),
        ),
        in_specs=[smem] * 3 + [hbm] * 9,
        out_specs=(hbm, hbm),
        scratch_shapes=[
            pltpu.VMEM((hidden_width, hidden), BF),
            pltpu.VMEM((hidden, cols), BF),
            pltpu.VMEM((hidden, cols), BF),
            pltpu.VMEM((seq_rows, model), BF),
            pltpu.VMEM((seq_rows, model), BF),
            [pltpu.VMEM((2, n_ctx, 2, HALF, w), BF) for w in widths],
            [pltpu.VMEM((n_ctx, 2, HALF, w), BF) for w in widths * 2],
            [pltpu.VMEM((n_sec, HALF, w), BF) for w in widths * 2],
            [pltpu.VMEM((n_sec, HALF, w), BF) for w in widths * 2],
            [pltpu.VMEM((n_ctx, 2, n_sec * HALF, w), BF) for w in widths],
            pltpu.VMEM((2, n_sec * HALF, hidden), F32),
            pltpu.VMEM((2, SIDE, 2, 2 * HALF, hidden), BF),
            pltpu.VMEM((2, SIDE, 2, 2 * HALF, hidden), BF),
            pltpu.VMEM((RING, 2, SIDE, 2, 2 * HALF, TILE), F32),
            pltpu.VMEM((tiles, 2, 2, 2 * HALF, TILE), BF),
            pltpu.VMEM((tiles, 2, 2, 2 * HALF, TILE), BF),
            pltpu.VMEM((tiles, 2, 2, 2, 2 * HALF, TILE), BF),
            pltpu.VMEM((tiles, 2, 2, 2, 2 * HALF, TILE), BF),
            pltpu.VMEM((tiles, block, TILE), BF),
            pltpu.VMEM((pieces, block, TILE), BF),
            pltpu.VMEM((pieces, block, TILE), BF),
            pltpu.VMEM((seq_rows, model), BF),
            pltpu.VMEM((2, block, 128), F32),
            pltpu.VMEM((SUBS, n_ctx, 2, 2, HALF, wide), BF),
            [pltpu.VMEM((n_ctx, 2, 2, HALF, wide), BF)] * SUBS,
            pltpu.VMEM((SUBS, n_sec, 2, HALF, wide), BF),
            [pltpu.VMEM((n_sec, 2, HALF, wide), BF)] * SUBS,
            pltpu.VMEM((SUBS, n_ctx, slot_count, own_images, wide), BF),
            pltpu.VMEM((SUBS, slot_count, own_images, wide), BF),
            pltpu.VMEM(patches.shape, BF),
            pltpu.VMEM(patch_gain.shape, F32),
            pltpu.VMEM((hidden,), F32),
            pltpu.VMEM((model,), F32),
            pltpu.VMEM((model,), F32),
            pltpu.VMEM((1, patch_gain.shape[0]), F32),
            pltpu.VMEM((1, hidden), F32),
            pltpu.VMEM((1, model), F32),
            pltpu.VMEM((1, model), F32),
            pltpu.SMEM((6, n_sec), jnp.int32),
            dma((10 + SUBS,)),
            dma((4,)),
            dma((4,)),
            dma((4,)),
            dma((4,)),
            dma((2, 4)),
            dma((2, 4)),
            dma((2, 4)),
            dma((2, 4)),
            dma((SIDE, 4)),
            dma((SIDE, 4)),
            dma,
            dma,
            dma((2,)),
            dma((2,)),
            dma((tiles, 2)),
            dma((tiles, 2)),
            dma((tiles, 2)),
            dma((tiles, 2)),
            dma((tiles,)),
            dma((tiles,)),
            dma((SUBS,)),
            dma((SUBS,)),
            dma((SUBS,)),
            dma((SUBS,)),
            dma((SUBS,)),
            dma((SUBS,)),
        ],
        compiler_params=pltpu.CompilerParams(
            collective_id=0, has_side_effects=True, vmem_limit_bytes=63 << 20
        ),
        name="merger",
    )(
        img_seq,
        img_off,
        img_cnt,
        patches,
        patch_gain,
        b_merge_in,
        b_merge_out,
        norm_gain,
        w_merge_in,
        w_merge_out,
        text_embed[0],
        upstream[0],
    )
    normed, grads = hand_over(normed, grads)
    return (normed[None], grads)


def solution(mesh):
    placed = (
        P(None, ("sec", "ctx"), None),
        P(),
        P(None, "ctx"),
        P("ctx"),
        P("ctx", None),
        P(),
        P("sec", "ctx", None),
        P(),
        P("sec", "ctx", None),
        P(),
        P(),
        P(),
    )
    return jax.shard_map(
        local,
        mesh=mesh,
        in_specs=placed,
        out_specs=(P("sec", "ctx", None), P(None, ("sec", "ctx"), None)),
        check_vma=False,
    )
```

```python
import jax
import jax.numpy as jnp
from jax import lax
from jax.experimental import pallas as pl
from jax.experimental.pallas import tpu as pltpu
from jax.sharding import PartitionSpec as P

MESH = pl.DeviceIdType.MESH
F32 = jnp.float32
BF = jnp.bfloat16
SIDE = 4
PIECES = 4
SUBS = 8
TAIL = 128
HALF = 16
TILE = 512
AHEAD = 4
RING = AHEAD + 2
LAGS = (4, 4)
EARLY = 2
PART_LAG = 3


def kernel(
    img_seq,
    img_off,
    img_cnt,
    patches_hbm,
    patch_gain_hbm,
    b_in_hbm,
    b_out_hbm,
    gain_hbm,
    w_in_hbm,
    w_out_hbm,
    text_hbm,
    up_hbm,
    normed_hbm,
    grad_hbm,
    w_in,
    w_tail,
    w_own,
    w_sib,
    text,
    up,
    xn,
    xr,
    ys,
    yr,
    xbuf,
    tail_n,
    ring,
    tail_s,
    tail_r,
    tail_x,
    acc,
    hid,
    hid_sib,
    sums,
    far_s,
    far_r,
    near_s,
    near_r,
    v_s,
    v,
    sus,
    nrm,
    stat,
    gs,
    gr,
    hs,
    hr,
    os_,
    own,
    patches,
    patch_gain_row,
    b_in_row,
    b_out_row,
    gain_row,
    patch_gain,
    b_in,
    b_out,
    gain,
    tab,
    loc,
    s_zs,
    r_zs,
    s_xy,
    r_xy,
    s_ag,
    r_ag,
    s_fw,
    r_fw,
    s_sib,
    r_sib,
    s_half,
    r_half,
    s_ring,
    r_ring,
    s_past,
    r_past,
    s_cross,
    r_cross,
    s_share,
    r_share,
    s_w,
    r_w,
    s_h,
    r_h,
    s_far,
    r_far,
    s_near,
    r_near,
    s_v,
    r_v,
    s_b1,
    r_b1,
    s_b2,
    r_b2,
    s_b3,
    r_b3,
):
    sec = lax.axis_index("sec")
    ctx = lax.axis_index("ctx")
    x, y = sec // SIDE, sec % SIDE
    z, k = ctx // 2, ctx % 2
    n_ctx = 2 * SIDE
    n_sec = SIDE * SIDE
    widths = [part.shape[-1] for part in xn]
    starts = [0, widths[0]]
    width = sum(widths) + TAIL
    halves = n_ctx // 2
    parts = 2 * len(widths)
    tiles = far_s.shape[0]
    pieces = sus.shape[0]

    def at_ctx(c):
        return {"sec": sec, "ctx": c}

    def at_sec(s):
        return {"sec": s, "ctx": ctx}

    def plane_peer(d):
        return ((x + d // SIDE) % SIDE) * SIDE + (y + d % SIDE) % SIDE

    up_z = at_ctx(((z + 1) % SIDE) * 2 + k)
    down_z = at_ctx(((z + SIDE - 1) % SIDE) * 2 + k)
    sib = at_ctx(z * 2 + 1 - k)

    def remote(src, dst, ssem, rsem, device):
        return pltpu.make_async_remote_copy(
            src_ref=src,
            dst_ref=dst,
            send_sem=ssem,
            recv_sem=rsem,
            device_id=device,
            device_id_type=MESH,
        )

    cols = w_own.shape[1]
    small = [
        pltpu.make_async_copy(src, dst, loc.at[5 + SUBS + i])
        for i, (src, dst) in enumerate(
            (
                (patches_hbm, patches),
                (patch_gain_hbm, patch_gain_row),
                (b_in_hbm, b_in_row),
                (b_out_hbm, b_out_row),
                (gain_hbm, gain_row),
            )
        )
    ]
    load_up = pltpu.make_async_copy(up_hbm, up, loc.at[0])
    load_text = pltpu.make_async_copy(text_hbm, text, loc.at[1])
    load_in = pltpu.make_async_copy(w_in_hbm, w_in, loc.at[2])
    load_tail = [
        pltpu.make_async_copy(
            w_in_hbm.at[pl.ds((b + 1) * width - TAIL, TAIL)],
            w_tail.at[b // halves, pl.ds((b % halves) * TAIL, TAIL)],
            loc.at[10 + SUBS + b],
        )
        for b in range(n_ctx)
    ]
    load_own = pltpu.make_async_copy(
        w_out_hbm.at[:, pl.ds(pl.multiple_of(k * cols, cols), cols)], w_own, loc.at[3]
    )

    barrier = pltpu.get_barrier_semaphore()

    def greet_ctx(d, carry):
        pl.semaphore_signal(
            barrier, inc=1, device_id=at_ctx((ctx + d) % n_ctx), device_id_type=MESH
        )
        return carry

    def greet_sec(d, carry):
        pl.semaphore_signal(barrier, inc=1, device_id=at_sec(plane_peer(d)), device_id_type=MESH)
        return carry

    lax.fori_loop(1, n_ctx, greet_ctx, 0)
    lax.fori_loop(1, n_sec, greet_sec, 0)
    for load in small:
        load.start()
    load_in.start()
    load_up.start()
    load_text.start()
    load_own.start()
    for load in load_tail:
        load.start()
    for load in small:
        load.wait()

    for row, line in (
        (patch_gain_row, patch_gain),
        (b_in_row, b_in),
        (b_out_row, b_out),
        (gain_row, gain),
    ):
        line[...] = row[...].reshape(line.shape)

    groups = patches.shape[2] // patch_gain.shape[1]
    group = patch_gain.shape[1]

    def norm_half(h):
        for i in range(2):
            for g in range(groups):
                f = patches[h * HALF : (h + 1) * HALF, i, pl.ds(g * group, group)].astype(F32)
                inv = lax.rsqrt(jnp.mean(f * f, axis=-1, keepdims=True) + 1e-06)
                f = (f * inv * patch_gain[...]).astype(BF)
                for b in range(group // width):
                    for part, start in zip(xn, starts):
                        at = b * width + start
                        part[h, g * (group // width) + b, i] = f[:, at : at + part.shape[-1]]
                    block_at = g * (group // width) + b
                    at = (block_at % halves) * TAIL
                    tail_n[block_at // halves, i, h * HALF : (h + 1) * HALF, at : at + TAIL] = f[
                        :, (b + 1) * width - TAIL : (b + 1) * width
                    ]

    def spread(u):
        h, mine = u // 2, xn[u % 2]

        def send_spread(d, carry):
            c = (ctx + d) % n_ctx
            remote(mine.at[h, c], xr[u].at[ctx], s_zs.at[u], r_zs.at[u], at_ctx(c)).start()
            return carry

        lax.fori_loop(1, n_ctx, send_spread, 0)
        xr[u][ctx] = mine[h, ctx]

    norm_half(0)
    pl.semaphore_wait(barrier, n_ctx + n_sec - 2)
    spread(0)
    spread(1)
    norm_half(1)
    spread(2)
    spread(3)

    def half_to_sib():
        return remote(tail_n.at[1 - k], ring.at[ctx], s_half, r_half, sib)

    half_to_sib().start()
    ring[ctx] = tail_n[k]
    send_w = remote(
        w_out_hbm.at[:, pl.ds(pl.multiple_of((1 - k) * cols, cols), cols)], w_sib, s_w, r_w, sib
    )

    def own_images(n, carry):
        tab[3, n] = img_seq[sec * n_sec + n]
        return carry

    def image_for(q, carry):
        found = jnp.int32(0)
        for n in range(n_sec):
            found = jnp.where(tab[3, n] == q, n, found)
        tab[0, q] = found
        return carry

    def image_from(g, carry):
        offset = jnp.int32(0)
        length = jnp.int32(0)
        for n in range(n_sec):
            hit = img_seq[g * n_sec + n] == sec
            offset = jnp.where(hit, img_off[g * n_sec + n], offset)
            length = jnp.where(hit, img_cnt[g * n_sec + n], length)
        tab[4, g] = offset
        tab[5, g] = length
        return carry

    def place_of(g, carry):
        before = jnp.int32(0)
        for n in range(n_sec):
            before = before + jnp.where(tab[4, n] < tab[4, g], 1, 0)
        tab[2, g] = before
        return carry

    def group_at(i, carry):
        found = jnp.int32(0)
        for n in range(n_sec):
            found = jnp.where(tab[2, n] == i, n, found)
        tab[1, i] = found
        return carry

    for fill in (own_images, image_for, image_from, place_of, group_at):
        lax.fori_loop(0, n_sec, fill, 0)

    def tail_along(c, way, ssem, rsem):
        part = ring.at[c]
        at = (way, c % 2)
        return remote(part, part, ssem.at[at], rsem.at[at], up_z if way == 0 else down_z)

    def tail_gather(chip, e, way):
        return tail_along(((z + chip) % SIDE) * 2 + e, way, s_ring, r_ring)

    def tail_forward(chip, e):
        return tail_along(((z + chip) % SIDE) * 2 + e, e, s_past, r_past)

    half_to_sib().wait_recv()
    for e in range(2):
        for way in range(2):
            tail_gather(0, e, way).start()

    def all_spread(u):
        most = pl.ds(0, n_ctx - 1)
        return remote(xn[u % 2].at[u // 2, most], xr[u].at[most], s_zs.at[u], r_zs.at[u], sib)

    def all_plane(u):
        most = pl.ds(0, n_sec - 1)
        return remote(ys[u].at[most], yr[u].at[most], s_xy.at[u], r_xy.at[u], sib)

    def to_plane(u):
        all_spread(u).wait_recv()

        def send_plane(d, carry):
            q = plane_peer(d)
            n = tab[0, q]
            ys[u][q] = xr[u][n // 2, n % 2]
            remote(ys[u].at[q], yr[u].at[sec], s_xy.at[u], r_xy.at[u], at_sec(q)).start()
            return carry

        lax.fori_loop(1, n_sec, send_plane, 0)
        n = tab[0, sec]
        yr[u][sec] = xr[u][n // 2, n % 2]

    rows = text.shape[0]
    first = [tab[4, tab[1, 2 * ctx + i]] - ctx * rows for i in range(2)]
    count = [tab[5, tab[1, 2 * ctx + i]] for i in range(2)]

    def placement(shape, slot_axis, row_axis):
        r = lax.broadcasted_iota(jnp.int32, shape, slot_axis)
        p = lax.broadcasted_iota(jnp.int32, shape, row_axis)
        slot = (r // (2 * HALF)) * HALF + r % HALF
        second = (r // HALF) % 2 == 1
        start = jnp.where(second, first[1], first[0])
        length = jnp.where(second, count[1], count[0])
        return jnp.where((slot < length) & (p == start + slot), 1.0, 0.0).astype(BF)

    def multiply(c, h, start=False):
        total = None if start else acc[h]
        for part, at in zip(xbuf, starts):
            rows_at = pl.ds(pl.multiple_of(c * width + at, 128), part.shape[-1])
            more = jnp.dot(part[c, h], w_in[rows_at, :], preferred_element_type=F32)
            total = more if total is None else total + more
        acc[h] = total

    c_down = ((z + SIDE - 1) % SIDE) * 2 + k
    c_up = ((z + 1) % SIDE) * 2 + k
    c_far = ((z + 2) % SIDE) * 2 + k

    def rows_of(c, u):
        return xbuf[u % 2].at[c, u // 2]

    def along(c, u, way, ssem, rsem):
        part = rows_of(c, u)
        return remote(part, part, ssem.at[way, u], rsem.at[way, u], up_z if way == 0 else down_z)

    def gather(c, u, way):
        return along(c, u, way, s_ag, r_ag)

    def forward(c, u, way):
        return along(c, u, way, s_fw, r_fw)

    def to_sib(c, u, rel):
        part = rows_of(c, u)
        return remote(part, part, s_sib.at[rel, u], r_sib.at[rel, u], sib)

    def other(c):
        return c + 1 - 2 * k

    ways = (0, 1, 1, 0)
    def to_ring(u):
        all_plane(u).wait_recv()
        for i in range(n_sec):
            xbuf[u % 2][ctx, u // 2, pl.ds(i * HALF, HALF), :] = yr[u][tab[1, i]]
        for way in range(2):
            gather(ctx, u, way).start()
        to_sib(ctx, u, 0).start()

    for n in range(parts + PART_LAG):
        if n < parts:
            to_plane(n)
        if n == parts - 1:
            for e in range(2):
                tail_gather(SIDE - 1 if e == 0 else 1, e, e).wait_recv()
                tail_forward(SIDE - 1 if e == 0 else 1, e).start()
        if n >= PART_LAG:
            to_ring(n - PART_LAG)

    def all_cross():
        most = pl.ds(0, n_sec - 1)
        return remote(tail_s.at[most], tail_r.at[most], s_cross, r_cross, sib)

    def tails_across():
        for e in range(2):
            tail_gather(SIDE - 1 if e == 1 else 1, e, 1 - e).wait_recv()
            tail_forward(2, e).wait_recv()

        def send(d, carry):
            q = plane_peer(d)
            n = tab[0, q]
            tail_s[q] = ring[n // 2, n % 2]
            remote(tail_s.at[q], tail_r.at[sec], s_cross, r_cross, at_sec(q)).start()
            return carry

        lax.fori_loop(1, n_sec, send, 0)
        n = tab[0, sec]
        tail_r[sec] = ring[n // 2, n % 2]

    def share_tails():
        return remote(tail_x.at[k], tail_x.at[k], s_share, r_share, sib)

    def place_tails():
        all_cross().wait_recv()
        for i in range(n_sec):
            rows_in = tail_r[tab[1, i]]
            for h in range(2):
                tail_x[k, h, pl.ds(i * HALF, HALF), :] = rows_in[h * HALF : (h + 1) * HALF]
        share_tails().start()

    def multiply_tails(side):
        for h in range(2):
            acc[h] += jnp.dot(tail_x[side, h], w_tail[side], preferred_element_type=F32)

    tails_across()
    send_w.start()
    load_in.wait()
    for load in load_tail:
        load.wait()
    for h in range(2):
        multiply(ctx, h, start=True)

    load_up.wait()
    pick = placement((4 * HALF, rows), 0, 1)

    def gather_upstream(j, carry):
        at = pl.ds(pl.multiple_of(j * TILE, TILE), TILE)
        sus[j] = jnp.dot(pick, up[:, at], preferred_element_type=F32).astype(BF)
        return carry

    lax.fori_loop(0, pieces, gather_upstream, 0)
    load_text.wait()

    def norm_text(b, carry):
        at = pl.ds(pl.multiple_of(b * HALF, HALF), HALF)
        t = text[at, :].astype(F32)
        inv = lax.rsqrt(jnp.mean(t * t, axis=-1, keepdims=True) + 1e-06)
        nrm[at, :] = (t * inv * gain[...]).astype(BF)
        return carry

    lax.fori_loop(0, rows // HALF, norm_text, 0)
    for h in range(2):
        for u in (2 * h, 2 * h + 1):
            for way, c, rel in ((0, c_down, 3), (1, c_up, 1)):
                gather(c, u, way).wait_recv()
                if ways[u] == way:
                    forward(c, u, way).start()
                to_sib(c, u, rel).start()
        for u in (2 * h, 2 * h + 1):
            to_sib(other(ctx), u, 0).wait_recv()
        multiply(other(ctx), h)
        multiply(c_down, h)
        multiply(c_up, h)
        for c, rel in ((c_down, 3), (c_up, 1)):
            for u in (2 * h, 2 * h + 1):
                to_sib(other(c), u, rel).wait_recv()
            multiply(other(c), h)
        if h == 0:
            place_tails()
            multiply_tails(k)
        else:
            remote(tail_x.at[1 - k], tail_x.at[1 - k], s_share, r_share, sib).wait_recv()
            multiply_tails(1 - k)

    def activate(h):
        def body(c, carry):
            at = pl.ds(pl.multiple_of(c * 2 * HALF, 2 * HALF), 2 * HALF)
            pre = acc[h, at, :] + b_in[...]
            act = 0.5 * pre * (1.0 + lax.erf(pre * (0.5**0.5)))
            rel = (c // 2 + SIDE - z) % SIDE
            hid[h, rel, c % 2] = act.astype(BF)
            return carry

        lax.fori_loop(0, n_ctx, body, 0)

    def send_h(h):
        return remote(hid.at[h], hid_sib.at[h], s_h.at[h], r_h.at[h], sib)

    def product(left, h, right, t):
        at = pl.ds(pl.multiple_of(t * TILE, TILE), TILE)
        out = jnp.dot(
            left[h].reshape(-1, left.shape[-1]), right[:, at], preferred_element_type=F32
        )
        return out.reshape(SIDE, 2, 2 * HALF, TILE)

    def far_half(t, way, h):
        return remote(
            far_s.at[t, way, h],
            far_r.at[t, way, h],
            s_far.at[t, way],
            r_far.at[t, way],
            up_z if way == 0 else down_z,
        )

    def early(h):
        send_h(h).wait_recv()
        for t in range(EARLY):
            sums[t, h] += product(hid_sib, h, w_sib, t)
            for way in range(2):
                far_s[t, way, h] = sums[t, h, 2, way].astype(BF)
                far_half(t, way, h).start()

    for h in range(2):
        for u in (2 * h, 2 * h + 1):
            forward(c_far, u, ways[u]).wait_recv()
            to_sib(c_far, u, 2).start()
        multiply(c_far, h)
        if h == 1:
            early(0)
        for u in (2 * h, 2 * h + 1):
            to_sib(other(c_far), u, 2).wait_recv()
        multiply(other(c_far), h)
        activate(h)
        send_h(h).start()
        if h == 0:
            load_own.wait()
            send_w.wait_recv()
        for t in range(EARLY):
            sums[t, h] = product(hid, h, w_own, t)
    early(1)

    def far(t, way):
        return remote(
            far_s.at[t, way],
            far_r.at[t, way],
            s_far.at[t, way],
            r_far.at[t, way],
            up_z if way == 0 else down_z,
        )

    def near(t, way):
        return remote(
            near_s.at[t, way],
            near_r.at[t, way],
            s_near.at[t, way],
            r_near.at[t, way],
            up_z if way == 0 else down_z,
        )

    def to_v(t):
        return remote(v_s.at[t], v.at[k * tiles + t], s_v.at[t], r_v.at[t], sib)

    def from_v(t):
        return remote(v_s.at[t], v.at[(1 - k) * tiles + t], s_v.at[t], r_v.at[t], sib)

    block = 4 * HALF

    def scatter_far(t):
        for way in range(2):
            far_s[t, way] = sums[t % RING, :, 2, way].astype(BF)
            far(t, way).start()

    def tally(j):
        val = v[j].astype(F32)
        scaled = sus[j].astype(F32) * gain[:, pl.ds(pl.multiple_of(j * TILE, TILE), TILE)]
        squares, inner = val * val, val * scaled
        for b in range(TILE // 128):
            stat[0] += squares[:, b * 128 : (b + 1) * 128]
            stat[1] += inner[:, b * 128 : (b + 1) * 128]

    stat[...] = jnp.zeros_like(stat)

    def step(t, carry):
        @pl.when(t < tiles)
        def _():
            for h in range(2):
                sums[t % RING, h] = product(hid, h, w_own, t) + product(hid_sib, h, w_sib, t)
            scatter_far(t)

        @pl.when((t >= AHEAD) & (t < tiles + AHEAD))
        def _():
            u = t - AHEAD
            for way, rel in ((0, 1), (1, 3)):
                far(u, way).wait_recv()
                near_s[u, way, way] = (
                    sums[u % RING, :, rel, way] + far_r[u, way].astype(F32)
                ).astype(BF)
                near_s[u, way, 1 - way] = sums[u % RING, :, rel, 1 - way].astype(BF)
                near(u, way).start()

        @pl.when((t > AHEAD) & (t <= tiles + AHEAD))
        def _():
            u = t - AHEAD - 1
            near(u, 0).wait_recv()
            near(u, 1).wait_recv()
            at = pl.ds(pl.multiple_of((k * tiles + u) * TILE, TILE), TILE)

            def whole(p):
                total = (
                    sums[u % RING, :, 0, p]
                    + near_r[u, 0, p].astype(F32)
                    + near_r[u, 1, p].astype(F32)
                )
                return (total.reshape(block, TILE) + b_out[:, at]).astype(BF)

            v_s[u] = whole(1 - k)
            to_v(u).start()
            v[k * tiles + u] = whole(k)
            tally(k * tiles + u)

        @pl.when(t > AHEAD + 1)
        def _():
            u = t - AHEAD - 2
            from_v(u).wait_recv()
            tally((1 - k) * tiles + u)

        return carry

    lax.fori_loop(EARLY, tiles + AHEAD + 1, step, 0)
    from_v(tiles - 1).wait_recv()
    tally((1 - k) * tiles + tiles - 1)

    model = pieces * TILE
    n_ctx_cols = model // n_ctx

    squares = jnp.sum(stat[0], axis=-1, keepdims=True)
    inner = jnp.sum(stat[1], axis=-1, keepdims=True)
    inv = lax.rsqrt(squares / model + 1e-06)
    pull = inv**3 * (inner / model)
    stat[0] = jnp.broadcast_to(inv, stat.shape[1:])
    stat[1] = jnp.broadcast_to(pull, stat.shape[1:])
    wide = gs.shape[-1]
    chunk = min(wide, TILE)

    def spread_back(sub, c):
        return remote(gs.at[sub, c], gr[sub].at[ctx], s_b1.at[sub], r_b1.at[sub], at_ctx(c))

    def gradient(sub, c, out):
        for b in range(wide // chunk):
            col = sub * wide + b * chunk
            j = c * (n_ctx_cols // TILE) + col // TILE
            at = pl.ds(pl.multiple_of(c * n_ctx_cols + col, chunk), chunk)
            inner = slice(col % TILE, col % TILE + chunk)
            scaled = sus[j, :, inner].astype(F32) * gain[:, at]
            val = stat[0, :, :1] * scaled - v[j, :, inner].astype(F32) * stat[1, :, :1]
            out[c, :, :, :, b * chunk : (b + 1) * chunk] = (
                val.astype(BF).reshape(2, 2, HALF, chunk)
            )

    def send_gradient(sub):
        def send_back(d, carry):
            c = (ctx + d) % n_ctx
            gradient(sub, c, gs.at[sub])
            spread_back(sub, c).start()
            return carry

        lax.fori_loop(1, n_ctx, send_back, 0)
        gradient(sub, ctx, gr[sub])

    put = placement((rows, block), 1, 0)
    row = lax.broadcasted_iota(jnp.int32, (rows, 1), 0)
    covered = ((row >= first[0]) & (row < first[0] + count[0])) | (
        (row >= first[1]) & (row < first[1] + count[1])
    )

    def put_images(j, carry):
        at = pl.ds(pl.multiple_of(j * TILE, TILE), TILE)
        image = (v[j].astype(F32) * stat[0, :, :1] * gain[:, at]).astype(BF)
        placed = jnp.dot(put, image, preferred_element_type=F32)
        nrm[:, at] = jnp.where(covered, placed, nrm[:, at].astype(F32)).astype(BF)
        return carry

    def exchange_back(sub):
        spread_sizes = pl.ds(0, n_ctx - 1)
        remote(
            gs.at[sub, spread_sizes], gr[sub].at[spread_sizes], s_b1.at[sub], r_b1.at[sub], sib
        ).wait_recv()

        def send(d, carry):
            s = plane_peer(d)
            n = tab[2, s]
            for h in range(2):
                hs[sub, s, h] = gr[sub][n // 2, h, n % 2]
            remote(hs.at[sub, s], hr[sub].at[sec], s_b2.at[sub], r_b2.at[sub], at_sec(s)).start()
            return carry

        lax.fori_loop(1, n_sec, send, 0)
        n = tab[2, sec]
        for h in range(2):
            hr[sub][sec, h] = gr[sub][n // 2, h, n % 2]

    def block_of(c, sub):
        return pl.ds(pl.multiple_of(c * n_ctx_cols + sub * wide, wide), wide)

    def home(sub, c):
        return remote(
            os_.at[sub, c],
            grad_hbm.at[:, :, block_of(ctx, sub)],
            s_b3.at[sub],
            r_b3.at[sub],
            at_ctx(c),
        )

    def collect(sub, c, out):
        for h in range(2):
            pair = [hr[sub][tab[3, 2 * c + i], h] for i in range(2)]
            out[h * HALF : (h + 1) * HALF] = jnp.stack(pair, axis=1)

    def keep(sub):
        return pltpu.make_async_copy(
            own.at[sub], grad_hbm.at[:, :, block_of(ctx, sub)], loc.at[5 + sub]
        )

    def exchange_home(sub):
        plane_sizes = pl.ds(0, n_sec - 1)
        remote(
            hs.at[sub, plane_sizes], hr[sub].at[plane_sizes], s_b2.at[sub], r_b2.at[sub], sib
        ).wait_recv()

        def send(d, carry):
            c = (ctx + d) % n_ctx
            collect(sub, c, os_.at[sub, c])
            home(sub, c).start()
            return carry

        lax.fori_loop(1, n_ctx, send, 0)
        collect(sub, ctx, own.at[sub])
        keep(sub).start()

    second, third = LAGS[0], sum(LAGS)
    done = 0
    for n in range(SUBS + third):
        if n < SUBS:
            send_gradient(n)
        if second <= n < SUBS + second:
            exchange_back(n - second)
        if n >= third:
            exchange_home(n - third)
        if n >= SUBS + second:
            upto = pieces * (n - SUBS - second + 1) // LAGS[1]
            lax.fori_loop(done, upto, put_images, 0)
            done = upto
    store_normed = pltpu.make_async_copy(nrm, normed_hbm, loc.at[4])
    store_normed.start()
    last = pl.ds(0, n_ctx - 1)

    def all_home(sub, part):
        return remote(part, part, s_b3.at[sub], r_b3.at[sub], sib)

    for sub in range(SUBS):
        all_home(sub, grad_hbm.at[:, :, pl.ds(0, (n_ctx - 1) * wide)]).wait_recv()

    for h in range(2):
        send_h(h).wait_send()
    for u in range(parts):
        all_spread(u).wait_send()
        all_plane(u).wait_send()
        for way in range(2):
            gather(ctx, u, way).wait_send()
        forward(ctx, u, ways[u]).wait_send()
        for rel in range(SIDE):
            to_sib(ctx, u, rel).wait_send()
    send_w.wait_send()
    half_to_sib().wait_send()
    for e in range(2):
        for way in range(2):
            tail_gather(0, e, way).wait_send()
        tail_forward(SIDE - 1 if e == 0 else 1, e).wait_send()
    all_cross().wait_send()
    share_tails().wait_send()

    def drain(t, carry):
        for way in range(2):
            far(t, way).wait_send()
            near(t, way).wait_send()
        to_v(t).wait_send()
        return carry

    lax.fori_loop(0, tiles, drain, 0)
    for sub in range(SUBS):
        plane = pl.ds(0, n_sec - 1)
        remote(gs.at[sub, last], gr[sub].at[last], s_b1.at[sub], r_b1.at[sub], sib).wait_send()
        remote(hs.at[sub, plane], hr[sub].at[plane], s_b2.at[sub], r_b2.at[sub], sib).wait_send()

        all_home(sub, os_.at[sub, last]).wait_send()
        keep(sub).wait()
    store_normed.wait()


def finish(normed_in, grads_in, normed_out, grads_out, normed, grads, sems):
    rows = normed.shape[0] // PIECES
    slots = grads.shape[0] // PIECES
    pairs = []
    for n in range(PIECES):
        at = pl.ds(n * rows, rows)
        pairs.append((normed_in.at[at], normed.at[at], normed_out.at[at]))
        at = pl.ds(n * slots, slots)
        pairs.append((grads_in.at[at], grads.at[at], grads_out.at[at]))
    loads = [
        pltpu.make_async_copy(a, b, sems.at[0, i]) for i, (a, b, _) in enumerate(pairs)
    ]
    stores = [
        pltpu.make_async_copy(b, c, sems.at[1, i]) for i, (_, b, c) in enumerate(pairs)
    ]
    for load in loads:
        load.start()
    for load, store in zip(loads, stores):
        load.wait()
        store.start()
    for store in stores:
        store.wait()


def hand_over(normed, grads):
    hbm = pl.BlockSpec(memory_space=pl.ANY)
    return pl.pallas_call(
        finish,
        out_shape=[jax.ShapeDtypeStruct(a.shape, a.dtype) for a in (normed, grads)],
        in_specs=[hbm] * 2,
        out_specs=[hbm] * 2,
        scratch_shapes=[
            pltpu.VMEM(normed.shape, normed.dtype),
            pltpu.VMEM(grads.shape, grads.dtype),
            pltpu.SemaphoreType.DMA((2, 2 * PIECES)),
        ],
        compiler_params=pltpu.CompilerParams(vmem_limit_bytes=63 << 20),
        name="finish",
    )(normed, grads)


def local(
    patches,
    patch_gain,
    w_merge_in,
    b_merge_in,
    w_merge_out,
    b_merge_out,
    text_embed,
    norm_gain,
    upstream,
    img_seq,
    img_off,
    img_cnt,
):
    slot_count, own_images, hidden_width = patches.shape
    n_sec = lax.axis_size("sec")
    n_ctx = lax.axis_size("ctx")
    seq_rows, model = text_embed.shape[1:]
    width = hidden_width // n_ctx
    widths = [(width - TAIL) // 2] * 2
    half_tail = n_ctx // 2 * TAIL
    hidden = w_merge_in.shape[1]
    cols = model // 2
    tiles = cols // TILE
    pieces = model // TILE
    wide = model // n_ctx // SUBS
    block = 4 * HALF
    smem = pl.BlockSpec(memory_space=pltpu.SMEM)
    vmem = pl.BlockSpec(memory_space=pltpu.VMEM)
    hbm = pl.BlockSpec(memory_space=pl.ANY)
    dma = pltpu.SemaphoreType.DMA
    normed, grads = pl.pallas_call(
        kernel,
        out_shape=(
            jax.ShapeDtypeStruct((seq_rows, model), BF),
            jax.ShapeDtypeStruct((slot_count, own_images, model), BF),
        ),
        in_specs=[smem] * 3 + [hbm] * 9,
        out_specs=(hbm, hbm),
        scratch_shapes=[
            pltpu.VMEM((hidden_width, hidden), BF),
            pltpu.VMEM((2, half_tail, hidden), BF),
            pltpu.VMEM((hidden, cols), BF),
            pltpu.VMEM((hidden, cols), BF),
            pltpu.VMEM((seq_rows, model), BF),
            pltpu.VMEM((seq_rows, model), BF),
            [pltpu.VMEM((2, n_ctx, 2, HALF, w), BF) for w in widths],
            [pltpu.VMEM((n_ctx, 2, HALF, w), BF) for w in widths * 2],
            [pltpu.VMEM((n_sec, HALF, w), BF) for w in widths * 2],
            [pltpu.VMEM((n_sec, HALF, w), BF) for w in widths * 2],
            [pltpu.VMEM((n_ctx, 2, n_sec * HALF, w), BF) for w in widths],
            pltpu.VMEM((2, own_images, slot_count, half_tail), BF),
            pltpu.VMEM((n_ctx, own_images, slot_count, half_tail), BF),
            pltpu.VMEM((n_sec, slot_count, half_tail), BF),
            pltpu.VMEM((n_sec, slot_count, half_tail), BF),
            pltpu.VMEM((2, 2, n_sec * HALF, half_tail), BF),
            pltpu.VMEM((2, n_sec * HALF, hidden), F32),
            pltpu.VMEM((2, SIDE, 2, 2 * HALF, hidden), BF),
            pltpu.VMEM((2, SIDE, 2, 2 * HALF, hidden), BF),
            pltpu.VMEM((RING, 2, SIDE, 2, 2 * HALF, TILE), F32),
            pltpu.VMEM((tiles, 2, 2, 2 * HALF, TILE), BF),
            pltpu.VMEM((tiles, 2, 2, 2 * HALF, TILE), BF),
            pltpu.VMEM((tiles, 2, 2, 2, 2 * HALF, TILE), BF),
            pltpu.VMEM((tiles, 2, 2, 2, 2 * HALF, TILE), BF),
            pltpu.VMEM((tiles, block, TILE), BF),
            pltpu.VMEM((pieces, block, TILE), BF),
            pltpu.VMEM((pieces, block, TILE), BF),
            pltpu.VMEM((seq_rows, model), BF),
            pltpu.VMEM((2, block, 128), F32),
            pltpu.VMEM((SUBS, n_ctx, 2, 2, HALF, wide), BF),
            [pltpu.VMEM((n_ctx, 2, 2, HALF, wide), BF)] * SUBS,
            pltpu.VMEM((SUBS, n_sec, 2, HALF, wide), BF),
            [pltpu.VMEM((n_sec, 2, HALF, wide), BF)] * SUBS,
            pltpu.VMEM((SUBS, n_ctx, slot_count, own_images, wide), BF),
            pltpu.VMEM((SUBS, slot_count, own_images, wide), BF),
            pltpu.VMEM(patches.shape, BF),
            pltpu.VMEM(patch_gain.shape, F32),
            pltpu.VMEM((hidden,), F32),
            pltpu.VMEM((model,), F32),
            pltpu.VMEM((model,), F32),
            pltpu.VMEM((1, patch_gain.shape[0]), F32),
            pltpu.VMEM((1, hidden), F32),
            pltpu.VMEM((1, model), F32),
            pltpu.VMEM((1, model), F32),
            pltpu.SMEM((6, n_sec), jnp.int32),
            dma((10 + SUBS + n_ctx,)),
            dma((4,)),
            dma((4,)),
            dma((4,)),
            dma((4,)),
            dma((2, 4)),
            dma((2, 4)),
            dma((2, 4)),
            dma((2, 4)),
            dma((SIDE, 4)),
            dma((SIDE, 4)),
            dma,
            dma,
            dma((2, 2)),
            dma((2, 2)),
            dma((2, 2)),
            dma((2, 2)),
            dma,
            dma,
            dma,
            dma,
            dma,
            dma,
            dma((2,)),
            dma((2,)),
            dma((tiles, 2)),
            dma((tiles, 2)),
            dma((tiles, 2)),
            dma((tiles, 2)),
            dma((tiles,)),
            dma((tiles,)),
            dma((SUBS,)),
            dma((SUBS,)),
            dma((SUBS,)),
            dma((SUBS,)),
            dma((SUBS,)),
            dma((SUBS,)),
        ],
        compiler_params=pltpu.CompilerParams(
            collective_id=0, has_side_effects=True, vmem_limit_bytes=63 << 20
        ),
        name="merger",
    )(
        img_seq,
        img_off,
        img_cnt,
        patches,
        patch_gain,
        b_merge_in,
        b_merge_out,
        norm_gain,
        w_merge_in,
        w_merge_out,
        text_embed[0],
        upstream[0],
    )
    normed, grads = hand_over(normed, grads)
    return (normed[None], grads)


def solution(mesh):
    placed = (
        P(None, ("sec", "ctx"), None),
        P(),
        P(None, "ctx"),
        P("ctx"),
        P("ctx", None),
        P(),
        P("sec", "ctx", None),
        P(),
        P("sec", "ctx", None),
        P(),
        P(),
        P(),
    )
    return jax.shard_map(
        local,
        mesh=mesh,
        in_specs=placed,
        out_specs=(P("sec", "ctx", None), P(None, ("sec", "ctx"), None)),
        check_vma=False,
    )
```

```python
import jax
import jax.numpy as jnp
from jax import lax
from jax.experimental import pallas as pl
from jax.experimental.pallas import tpu as pltpu
from jax.sharding import PartitionSpec as P

MESH = pl.DeviceIdType.MESH
F32 = jnp.float32
BF = jnp.bfloat16
SIDE = 4
PIECES = 4
SUBS = 8
TAIL = 128
HALF = 16
TILE = 512
AHEAD = 4
RING = AHEAD + 2
LAGS = (4, 4)
EARLY = 2
PART_LAG = 3


def kernel(
    img_seq,
    img_off,
    img_cnt,
    patches_hbm,
    patch_gain_hbm,
    b_in_hbm,
    b_out_hbm,
    gain_hbm,
    w_in_hbm,
    w_out_hbm,
    text_hbm,
    up_hbm,
    normed_hbm,
    grad_hbm,
    w_in,
    w_tail,
    w_own,
    w_sib,
    text,
    up,
    xn,
    xr,
    ys,
    yr,
    xbuf,
    tail_n,
    ring,
    tail_s,
    tail_r,
    tail_x,
    acc,
    hid,
    hid_sib,
    sums,
    far_s,
    far_r,
    near_s,
    near_r,
    v_s,
    v,
    sus,
    nrm,
    stat,
    gs,
    gr,
    hs,
    hr,
    os_,
    own,
    patches,
    patch_gain_row,
    b_in_row,
    b_out_row,
    gain_row,
    patch_gain,
    b_in,
    b_out,
    gain,
    tab,
    loc,
    s_zs,
    r_zs,
    s_xy,
    r_xy,
    s_ag,
    r_ag,
    s_fw,
    r_fw,
    s_sib,
    r_sib,
    s_half,
    r_half,
    s_ring,
    r_ring,
    s_past,
    r_past,
    s_cross,
    r_cross,
    s_share,
    r_share,
    s_w,
    r_w,
    s_h,
    r_h,
    s_far,
    r_far,
    s_near,
    r_near,
    s_v,
    r_v,
    s_b1,
    r_b1,
    s_b2,
    r_b2,
    s_b3,
    r_b3,
):
    sec = lax.axis_index("sec")
    ctx = lax.axis_index("ctx")
    x, y = sec // SIDE, sec % SIDE
    z, k = ctx // 2, ctx % 2
    n_ctx = 2 * SIDE
    n_sec = SIDE * SIDE
    widths = [part.shape[-1] for part in xn]
    starts = [0, widths[0]]
    width = sum(widths) + TAIL
    halves = n_ctx // 2
    parts = 2 * len(widths)
    tiles = far_s.shape[0]
    pieces = sus.shape[0]

    def at_ctx(c):
        return {"sec": sec, "ctx": c}

    def at_sec(s):
        return {"sec": s, "ctx": ctx}

    def far_first(d, n):
        return 1 + (d + n // 2 - 2) % (n - 1)

    def plane_peer(d):
        d = far_first(d, n_sec)
        return ((x + d // SIDE) % SIDE) * SIDE + (y + d % SIDE) % SIDE

    up_z = at_ctx(((z + 1) % SIDE) * 2 + k)
    down_z = at_ctx(((z + SIDE - 1) % SIDE) * 2 + k)
    sib = at_ctx(z * 2 + 1 - k)

    def remote(src, dst, ssem, rsem, device):
        return pltpu.make_async_remote_copy(
            src_ref=src,
            dst_ref=dst,
            send_sem=ssem,
            recv_sem=rsem,
            device_id=device,
            device_id_type=MESH,
        )

    cols = w_own.shape[1]
    small = [
        pltpu.make_async_copy(src, dst, loc.at[5 + SUBS + i])
        for i, (src, dst) in enumerate(
            (
                (patches_hbm, patches),
                (patch_gain_hbm, patch_gain_row),
                (b_in_hbm, b_in_row),
                (b_out_hbm, b_out_row),
                (gain_hbm, gain_row),
            )
        )
    ]
    load_up = pltpu.make_async_copy(up_hbm, up, loc.at[0])
    load_text = pltpu.make_async_copy(text_hbm, text, loc.at[1])
    load_in = pltpu.make_async_copy(w_in_hbm, w_in, loc.at[2])
    load_tail = [
        pltpu.make_async_copy(
            w_in_hbm.at[pl.ds((b + 1) * width - TAIL, TAIL)],
            w_tail.at[b // halves, pl.ds((b % halves) * TAIL, TAIL)],
            loc.at[10 + SUBS + b],
        )
        for b in range(n_ctx)
    ]
    load_own = pltpu.make_async_copy(
        w_out_hbm.at[:, pl.ds(pl.multiple_of(k * cols, cols), cols)], w_own, loc.at[3]
    )

    barrier = pltpu.get_barrier_semaphore()

    def greet_ctx(d, carry):
        pl.semaphore_signal(
            barrier, inc=1, device_id=at_ctx((ctx + d) % n_ctx), device_id_type=MESH
        )
        return carry

    def greet_sec(d, carry):
        pl.semaphore_signal(barrier, inc=1, device_id=at_sec(plane_peer(d)), device_id_type=MESH)
        return carry

    lax.fori_loop(1, n_ctx, greet_ctx, 0)
    lax.fori_loop(1, n_sec, greet_sec, 0)
    for load in small:
        load.start()
    load_in.start()
    load_up.start()
    load_text.start()
    load_own.start()
    for load in load_tail:
        load.start()
    for load in small:
        load.wait()

    for row, line in (
        (patch_gain_row, patch_gain),
        (b_in_row, b_in),
        (b_out_row, b_out),
        (gain_row, gain),
    ):
        line[...] = row[...].reshape(line.shape)

    groups = patches.shape[2] // patch_gain.shape[1]
    group = patch_gain.shape[1]

    def norm_half(h):
        for i in range(2):
            for g in range(groups):
                f = patches[h * HALF : (h + 1) * HALF, i, pl.ds(g * group, group)].astype(F32)
                inv = lax.rsqrt(jnp.mean(f * f, axis=-1, keepdims=True) + 1e-06)
                f = (f * inv * patch_gain[...]).astype(BF)
                for b in range(group // width):
                    for part, start in zip(xn, starts):
                        at = b * width + start
                        part[h, g * (group // width) + b, i] = f[:, at : at + part.shape[-1]]
                    block_at = g * (group // width) + b
                    at = (block_at % halves) * TAIL
                    tail_n[block_at // halves, i, h * HALF : (h + 1) * HALF, at : at + TAIL] = f[
                        :, (b + 1) * width - TAIL : (b + 1) * width
                    ]

    def spread(u):
        h, mine = u // 2, xn[u % 2]

        def send_spread(d, carry):
            c = (ctx + far_first(d, n_ctx)) % n_ctx
            remote(mine.at[h, c], xr[u].at[ctx], s_zs.at[u], r_zs.at[u], at_ctx(c)).start()
            return carry

        lax.fori_loop(1, n_ctx, send_spread, 0)
        xr[u][ctx] = mine[h, ctx]

    norm_half(0)
    pl.semaphore_wait(barrier, n_ctx + n_sec - 2)
    spread(0)
    spread(1)
    norm_half(1)
    spread(2)
    spread(3)

    def half_to_sib():
        return remote(tail_n.at[1 - k], ring.at[ctx], s_half, r_half, sib)

    half_to_sib().start()
    ring[ctx] = tail_n[k]
    send_w = remote(
        w_out_hbm.at[:, pl.ds(pl.multiple_of((1 - k) * cols, cols), cols)], w_sib, s_w, r_w, sib
    )

    def own_images(n, carry):
        tab[3, n] = img_seq[sec * n_sec + n]
        return carry

    def image_for(q, carry):
        found = jnp.int32(0)
        for n in range(n_sec):
            found = jnp.where(tab[3, n] == q, n, found)
        tab[0, q] = found
        return carry

    def image_from(g, carry):
        offset = jnp.int32(0)
        length = jnp.int32(0)
        for n in range(n_sec):
            hit = img_seq[g * n_sec + n] == sec
            offset = jnp.where(hit, img_off[g * n_sec + n], offset)
            length = jnp.where(hit, img_cnt[g * n_sec + n], length)
        tab[4, g] = offset
        tab[5, g] = length
        return carry

    def place_of(g, carry):
        before = jnp.int32(0)
        for n in range(n_sec):
            before = before + jnp.where(tab[4, n] < tab[4, g], 1, 0)
        tab[2, g] = before
        return carry

    def group_at(i, carry):
        found = jnp.int32(0)
        for n in range(n_sec):
            found = jnp.where(tab[2, n] == i, n, found)
        tab[1, i] = found
        return carry

    for fill in (own_images, image_for, image_from, place_of, group_at):
        lax.fori_loop(0, n_sec, fill, 0)

    def tail_along(c, way, ssem, rsem):
        part = ring.at[c]
        at = (way, c % 2)
        return remote(part, part, ssem.at[at], rsem.at[at], up_z if way == 0 else down_z)

    def tail_gather(chip, e, way):
        return tail_along(((z + chip) % SIDE) * 2 + e, way, s_ring, r_ring)

    def tail_forward(chip, e):
        return tail_along(((z + chip) % SIDE) * 2 + e, e, s_past, r_past)

    half_to_sib().wait_recv()
    for e in range(2):
        for way in range(2):
            tail_gather(0, e, way).start()

    def all_spread(u):
        most = pl.ds(0, n_ctx - 1)
        return remote(xn[u % 2].at[u // 2, most], xr[u].at[most], s_zs.at[u], r_zs.at[u], sib)

    def all_plane(u):
        most = pl.ds(0, n_sec - 1)
        return remote(ys[u].at[most], yr[u].at[most], s_xy.at[u], r_xy.at[u], sib)

    def to_plane(u):
        all_spread(u).wait_recv()

        def send_plane(d, carry):
            q = plane_peer(d)
            n = tab[0, q]
            ys[u][q] = xr[u][n // 2, n % 2]
            remote(ys[u].at[q], yr[u].at[sec], s_xy.at[u], r_xy.at[u], at_sec(q)).start()
            return carry

        lax.fori_loop(1, n_sec, send_plane, 0)
        n = tab[0, sec]
        yr[u][sec] = xr[u][n // 2, n % 2]

    rows = text.shape[0]
    first = [tab[4, tab[1, 2 * ctx + i]] - ctx * rows for i in range(2)]
    count = [tab[5, tab[1, 2 * ctx + i]] for i in range(2)]

    def placement(shape, slot_axis, row_axis):
        r = lax.broadcasted_iota(jnp.int32, shape, slot_axis)
        p = lax.broadcasted_iota(jnp.int32, shape, row_axis)
        slot = (r // (2 * HALF)) * HALF + r % HALF
        second = (r // HALF) % 2 == 1
        start = jnp.where(second, first[1], first[0])
        length = jnp.where(second, count[1], count[0])
        return jnp.where((slot < length) & (p == start + slot), 1.0, 0.0).astype(BF)

    def multiply(c, h, start=False):
        total = None if start else acc[h]
        for part, at in zip(xbuf, starts):
            rows_at = pl.ds(pl.multiple_of(c * width + at, 128), part.shape[-1])
            more = jnp.dot(part[c, h], w_in[rows_at, :], preferred_element_type=F32)
            total = more if total is None else total + more
        acc[h] = total

    c_down = ((z + SIDE - 1) % SIDE) * 2 + k
    c_up = ((z + 1) % SIDE) * 2 + k
    c_far = ((z + 2) % SIDE) * 2 + k

    def rows_of(c, u):
        return xbuf[u % 2].at[c, u // 2]

    def along(c, u, way, ssem, rsem):
        part = rows_of(c, u)
        return remote(part, part, ssem.at[way, u], rsem.at[way, u], up_z if way == 0 else down_z)

    def gather(c, u, way):
        return along(c, u, way, s_ag, r_ag)

    def forward(c, u, way):
        return along(c, u, way, s_fw, r_fw)

    def to_sib(c, u, rel):
        part = rows_of(c, u)
        return remote(part, part, s_sib.at[rel, u], r_sib.at[rel, u], sib)

    def other(c):
        return c + 1 - 2 * k

    ways = (0, 1, 1, 0)
    def to_ring(u):
        all_plane(u).wait_recv()
        for i in range(n_sec):
            xbuf[u % 2][ctx, u // 2, pl.ds(i * HALF, HALF), :] = yr[u][tab[1, i]]
        for way in range(2):
            gather(ctx, u, way).start()
        to_sib(ctx, u, 0).start()

    for n in range(parts + PART_LAG):
        if n < parts:
            to_plane(n)
        if n == parts - 1:
            for e in range(2):
                tail_gather(SIDE - 1 if e == 0 else 1, e, e).wait_recv()
                tail_forward(SIDE - 1 if e == 0 else 1, e).start()
        if n >= PART_LAG:
            to_ring(n - PART_LAG)

    def all_cross():
        most = pl.ds(0, n_sec - 1)
        return remote(tail_s.at[most], tail_r.at[most], s_cross, r_cross, sib)

    def tails_across():
        for e in range(2):
            tail_gather(SIDE - 1 if e == 1 else 1, e, 1 - e).wait_recv()
            tail_forward(2, e).wait_recv()

        def send(d, carry):
            q = plane_peer(d)
            n = tab[0, q]
            tail_s[q] = ring[n // 2, n % 2]
            remote(tail_s.at[q], tail_r.at[sec], s_cross, r_cross, at_sec(q)).start()
            return carry

        lax.fori_loop(1, n_sec, send, 0)
        n = tab[0, sec]
        tail_r[sec] = ring[n // 2, n % 2]

    def share_tails():
        return remote(tail_x.at[k], tail_x.at[k], s_share, r_share, sib)

    def place_tails():
        all_cross().wait_recv()
        for i in range(n_sec):
            rows_in = tail_r[tab[1, i]]
            for h in range(2):
                tail_x[k, h, pl.ds(i * HALF, HALF), :] = rows_in[h * HALF : (h + 1) * HALF]
        share_tails().start()

    def multiply_tails(side):
        for h in range(2):
            acc[h] += jnp.dot(tail_x[side, h], w_tail[side], preferred_element_type=F32)

    tails_across()
    send_w.start()
    load_in.wait()
    for load in load_tail:
        load.wait()
    for h in range(2):
        multiply(ctx, h, start=True)

    load_up.wait()
    pick = placement((4 * HALF, rows), 0, 1)

    def gather_upstream(j, carry):
        at = pl.ds(pl.multiple_of(j * TILE, TILE), TILE)
        sus[j] = jnp.dot(pick, up[:, at], preferred_element_type=F32).astype(BF)
        return carry

    lax.fori_loop(0, pieces, gather_upstream, 0)
    load_text.wait()

    def norm_text(b, carry):
        at = pl.ds(pl.multiple_of(b * HALF, HALF), HALF)
        t = text[at, :].astype(F32)
        inv = lax.rsqrt(jnp.mean(t * t, axis=-1, keepdims=True) + 1e-06)
        nrm[at, :] = (t * inv * gain[...]).astype(BF)
        return carry

    lax.fori_loop(0, rows // HALF, norm_text, 0)
    for h in range(2):
        for u in (2 * h, 2 * h + 1):
            for way, c, rel in ((0, c_down, 3), (1, c_up, 1)):
                gather(c, u, way).wait_recv()
                if ways[u] == way:
                    forward(c, u, way).start()
                to_sib(c, u, rel).start()
        for u in (2 * h, 2 * h + 1):
            to_sib(other(ctx), u, 0).wait_recv()
        multiply(other(ctx), h)
        multiply(c_down, h)
        multiply(c_up, h)
        for c, rel in ((c_down, 3), (c_up, 1)):
            for u in (2 * h, 2 * h + 1):
                to_sib(other(c), u, rel).wait_recv()
            multiply(other(c), h)
        if h == 0:
            place_tails()
            multiply_tails(k)
        else:
            remote(tail_x.at[1 - k], tail_x.at[1 - k], s_share, r_share, sib).wait_recv()
            multiply_tails(1 - k)

    def activate(h):
        def body(c, carry):
            at = pl.ds(pl.multiple_of(c * 2 * HALF, 2 * HALF), 2 * HALF)
            pre = acc[h, at, :] + b_in[...]
            act = 0.5 * pre * (1.0 + lax.erf(pre * (0.5**0.5)))
            rel = (c // 2 + SIDE - z) % SIDE
            hid[h, rel, c % 2] = act.astype(BF)
            return carry

        lax.fori_loop(0, n_ctx, body, 0)

    def send_h(h):
        return remote(hid.at[h], hid_sib.at[h], s_h.at[h], r_h.at[h], sib)

    def product(left, h, right, t):
        at = pl.ds(pl.multiple_of(t * TILE, TILE), TILE)
        out = jnp.dot(
            left[h].reshape(-1, left.shape[-1]), right[:, at], preferred_element_type=F32
        )
        return out.reshape(SIDE, 2, 2 * HALF, TILE)

    def far_half(t, way, h):
        return remote(
            far_s.at[t, way, h],
            far_r.at[t, way, h],
            s_far.at[t, way],
            r_far.at[t, way],
            up_z if way == 0 else down_z,
        )

    def early(h):
        send_h(h).wait_recv()
        for t in range(EARLY):
            sums[t, h] += product(hid_sib, h, w_sib, t)
            for way in range(2):
                far_s[t, way, h] = sums[t, h, 2, way].astype(BF)
                far_half(t, way, h).start()

    for h in range(2):
        for u in (2 * h, 2 * h + 1):
            forward(c_far, u, ways[u]).wait_recv()
            to_sib(c_far, u, 2).start()
        multiply(c_far, h)
        if h == 1:
            early(0)
        for u in (2 * h, 2 * h + 1):
            to_sib(other(c_far), u, 2).wait_recv()
        multiply(other(c_far), h)
        activate(h)
        send_h(h).start()
        if h == 0:
            load_own.wait()
            send_w.wait_recv()
        for t in range(EARLY):
            sums[t, h] = product(hid, h, w_own, t)
    early(1)

    def far(t, way):
        return remote(
            far_s.at[t, way],
            far_r.at[t, way],
            s_far.at[t, way],
            r_far.at[t, way],
            up_z if way == 0 else down_z,
        )

    def near(t, way):
        return remote(
            near_s.at[t, way],
            near_r.at[t, way],
            s_near.at[t, way],
            r_near.at[t, way],
            up_z if way == 0 else down_z,
        )

    def to_v(t):
        return remote(v_s.at[t], v.at[k * tiles + t], s_v.at[t], r_v.at[t], sib)

    def from_v(t):
        return remote(v_s.at[t], v.at[(1 - k) * tiles + t], s_v.at[t], r_v.at[t], sib)

    block = 4 * HALF

    def scatter_far(t):
        for way in range(2):
            far_s[t, way] = sums[t % RING, :, 2, way].astype(BF)
            far(t, way).start()

    def tally(j):
        val = v[j].astype(F32)
        scaled = sus[j].astype(F32) * gain[:, pl.ds(pl.multiple_of(j * TILE, TILE), TILE)]
        squares, inner = val * val, val * scaled
        for b in range(TILE // 128):
            stat[0] += squares[:, b * 128 : (b + 1) * 128]
            stat[1] += inner[:, b * 128 : (b + 1) * 128]

    stat[...] = jnp.zeros_like(stat)

    def step(t, carry):
        @pl.when(t < tiles)
        def _():
            for h in range(2):
                sums[t % RING, h] = product(hid, h, w_own, t) + product(hid_sib, h, w_sib, t)
            scatter_far(t)

        @pl.when((t >= AHEAD) & (t < tiles + AHEAD))
        def _():
            u = t - AHEAD
            for way, rel in ((0, 1), (1, 3)):
                far(u, way).wait_recv()
                near_s[u, way, way] = (
                    sums[u % RING, :, rel, way] + far_r[u, way].astype(F32)
                ).astype(BF)
                near_s[u, way, 1 - way] = sums[u % RING, :, rel, 1 - way].astype(BF)
                near(u, way).start()

        @pl.when((t > AHEAD) & (t <= tiles + AHEAD))
        def _():
            u = t - AHEAD - 1
            near(u, 0).wait_recv()
            near(u, 1).wait_recv()
            at = pl.ds(pl.multiple_of((k * tiles + u) * TILE, TILE), TILE)

            def whole(p):
                total = (
                    sums[u % RING, :, 0, p]
                    + near_r[u, 0, p].astype(F32)
                    + near_r[u, 1, p].astype(F32)
                )
                return (total.reshape(block, TILE) + b_out[:, at]).astype(BF)

            v_s[u] = whole(1 - k)
            to_v(u).start()
            v[k * tiles + u] = whole(k)
            tally(k * tiles + u)

        @pl.when(t > AHEAD + 1)
        def _():
            u = t - AHEAD - 2
            from_v(u).wait_recv()
            tally((1 - k) * tiles + u)

        return carry

    lax.fori_loop(EARLY, tiles + AHEAD + 1, step, 0)
    from_v(tiles - 1).wait_recv()
    tally((1 - k) * tiles + tiles - 1)

    model = pieces * TILE
    n_ctx_cols = model // n_ctx

    squares = jnp.sum(stat[0], axis=-1, keepdims=True)
    inner = jnp.sum(stat[1], axis=-1, keepdims=True)
    inv = lax.rsqrt(squares / model + 1e-06)
    pull = inv**3 * (inner / model)
    stat[0] = jnp.broadcast_to(inv, stat.shape[1:])
    stat[1] = jnp.broadcast_to(pull, stat.shape[1:])
    wide = gs.shape[-1]
    chunk = min(wide, TILE)

    def spread_back(sub, c):
        return remote(gs.at[sub, c], gr[sub].at[ctx], s_b1.at[sub], r_b1.at[sub], at_ctx(c))

    def gradient(sub, c, out):
        for b in range(wide // chunk):
            col = sub * wide + b * chunk
            j = c * (n_ctx_cols // TILE) + col // TILE
            at = pl.ds(pl.multiple_of(c * n_ctx_cols + col, chunk), chunk)
            inner = slice(col % TILE, col % TILE + chunk)
            scaled = sus[j, :, inner].astype(F32) * gain[:, at]
            val = stat[0, :, :1] * scaled - v[j, :, inner].astype(F32) * stat[1, :, :1]
            out[c, :, :, :, b * chunk : (b + 1) * chunk] = (
                val.astype(BF).reshape(2, 2, HALF, chunk)
            )

    def send_gradient(sub):
        def send_back(d, carry):
            c = (ctx + far_first(d, n_ctx)) % n_ctx
            gradient(sub, c, gs.at[sub])
            spread_back(sub, c).start()
            return carry

        lax.fori_loop(1, n_ctx, send_back, 0)
        gradient(sub, ctx, gr[sub])

    put = placement((rows, block), 1, 0)
    row = lax.broadcasted_iota(jnp.int32, (rows, 1), 0)
    covered = ((row >= first[0]) & (row < first[0] + count[0])) | (
        (row >= first[1]) & (row < first[1] + count[1])
    )

    def put_images(j, carry):
        at = pl.ds(pl.multiple_of(j * TILE, TILE), TILE)
        image = (v[j].astype(F32) * stat[0, :, :1] * gain[:, at]).astype(BF)
        placed = jnp.dot(put, image, preferred_element_type=F32)
        nrm[:, at] = jnp.where(covered, placed, nrm[:, at].astype(F32)).astype(BF)
        return carry

    def exchange_back(sub):
        spread_sizes = pl.ds(0, n_ctx - 1)
        remote(
            gs.at[sub, spread_sizes], gr[sub].at[spread_sizes], s_b1.at[sub], r_b1.at[sub], sib
        ).wait_recv()

        def send(d, carry):
            s = plane_peer(d)
            n = tab[2, s]
            for h in range(2):
                hs[sub, s, h] = gr[sub][n // 2, h, n % 2]
            remote(hs.at[sub, s], hr[sub].at[sec], s_b2.at[sub], r_b2.at[sub], at_sec(s)).start()
            return carry

        lax.fori_loop(1, n_sec, send, 0)
        n = tab[2, sec]
        for h in range(2):
            hr[sub][sec, h] = gr[sub][n // 2, h, n % 2]

    def block_of(c, sub):
        return pl.ds(pl.multiple_of(c * n_ctx_cols + sub * wide, wide), wide)

    def home(sub, c):
        return remote(
            os_.at[sub, c],
            grad_hbm.at[:, :, block_of(ctx, sub)],
            s_b3.at[sub],
            r_b3.at[sub],
            at_ctx(c),
        )

    def collect(sub, c, out):
        for h in range(2):
            pair = [hr[sub][tab[3, 2 * c + i], h] for i in range(2)]
            out[h * HALF : (h + 1) * HALF] = jnp.stack(pair, axis=1)

    def keep(sub):
        return pltpu.make_async_copy(
            own.at[sub], grad_hbm.at[:, :, block_of(ctx, sub)], loc.at[5 + sub]
        )

    def exchange_home(sub):
        plane_sizes = pl.ds(0, n_sec - 1)
        remote(
            hs.at[sub, plane_sizes], hr[sub].at[plane_sizes], s_b2.at[sub], r_b2.at[sub], sib
        ).wait_recv()

        def send(d, carry):
            c = (ctx + far_first(d, n_ctx)) % n_ctx
            collect(sub, c, os_.at[sub, c])
            home(sub, c).start()
            return carry

        lax.fori_loop(1, n_ctx, send, 0)
        collect(sub, ctx, own.at[sub])
        keep(sub).start()

    second, third = LAGS[0], sum(LAGS)
    done = 0
    for n in range(SUBS + third):
        if n < SUBS:
            send_gradient(n)
        if second <= n < SUBS + second:
            exchange_back(n - second)
        if n >= third:
            exchange_home(n - third)
        if n >= SUBS + second:
            upto = pieces * (n - SUBS - second + 1) // LAGS[1]
            lax.fori_loop(done, upto, put_images, 0)
            done = upto
    store_normed = pltpu.make_async_copy(nrm, normed_hbm, loc.at[4])
    store_normed.start()
    last = pl.ds(0, n_ctx - 1)

    def all_home(sub, part):
        return remote(part, part, s_b3.at[sub], r_b3.at[sub], sib)

    for sub in range(SUBS):
        all_home(sub, grad_hbm.at[:, :, pl.ds(0, (n_ctx - 1) * wide)]).wait_recv()

    for h in range(2):
        send_h(h).wait_send()
    for u in range(parts):
        all_spread(u).wait_send()
        all_plane(u).wait_send()
        for way in range(2):
            gather(ctx, u, way).wait_send()
        forward(ctx, u, ways[u]).wait_send()
        for rel in range(SIDE):
            to_sib(ctx, u, rel).wait_send()
    send_w.wait_send()
    half_to_sib().wait_send()
    for e in range(2):
        for way in range(2):
            tail_gather(0, e, way).wait_send()
        tail_forward(SIDE - 1 if e == 0 else 1, e).wait_send()
    all_cross().wait_send()
    share_tails().wait_send()

    def drain(t, carry):
        for way in range(2):
            far(t, way).wait_send()
            near(t, way).wait_send()
        to_v(t).wait_send()
        return carry

    lax.fori_loop(0, tiles, drain, 0)
    for sub in range(SUBS):
        plane = pl.ds(0, n_sec - 1)
        remote(gs.at[sub, last], gr[sub].at[last], s_b1.at[sub], r_b1.at[sub], sib).wait_send()
        remote(hs.at[sub, plane], hr[sub].at[plane], s_b2.at[sub], r_b2.at[sub], sib).wait_send()

        all_home(sub, os_.at[sub, last]).wait_send()
        keep(sub).wait()
    store_normed.wait()


def finish(normed_in, grads_in, normed_out, grads_out, normed, grads, sems):
    rows = normed.shape[0] // PIECES
    slots = grads.shape[0] // PIECES
    pairs = []
    for n in range(PIECES):
        at = pl.ds(n * rows, rows)
        pairs.append((normed_in.at[at], normed.at[at], normed_out.at[at]))
        at = pl.ds(n * slots, slots)
        pairs.append((grads_in.at[at], grads.at[at], grads_out.at[at]))
    loads = [
        pltpu.make_async_copy(a, b, sems.at[0, i]) for i, (a, b, _) in enumerate(pairs)
    ]
    stores = [
        pltpu.make_async_copy(b, c, sems.at[1, i]) for i, (_, b, c) in enumerate(pairs)
    ]
    for load in loads:
        load.start()
    for load, store in zip(loads, stores):
        load.wait()
        store.start()
    for store in stores:
        store.wait()


def hand_over(normed, grads):
    hbm = pl.BlockSpec(memory_space=pl.ANY)
    return pl.pallas_call(
        finish,
        out_shape=[jax.ShapeDtypeStruct(a.shape, a.dtype) for a in (normed, grads)],
        in_specs=[hbm] * 2,
        out_specs=[hbm] * 2,
        scratch_shapes=[
            pltpu.VMEM(normed.shape, normed.dtype),
            pltpu.VMEM(grads.shape, grads.dtype),
            pltpu.SemaphoreType.DMA((2, 2 * PIECES)),
        ],
        compiler_params=pltpu.CompilerParams(vmem_limit_bytes=63 << 20),
        name="finish",
    )(normed, grads)


def local(
    patches,
    patch_gain,
    w_merge_in,
    b_merge_in,
    w_merge_out,
    b_merge_out,
    text_embed,
    norm_gain,
    upstream,
    img_seq,
    img_off,
    img_cnt,
):
    slot_count, own_images, hidden_width = patches.shape
    n_sec = lax.axis_size("sec")
    n_ctx = lax.axis_size("ctx")
    seq_rows, model = text_embed.shape[1:]
    width = hidden_width // n_ctx
    widths = [(width - TAIL) // 2] * 2
    half_tail = n_ctx // 2 * TAIL
    hidden = w_merge_in.shape[1]
    cols = model // 2
    tiles = cols // TILE
    pieces = model // TILE
    wide = model // n_ctx // SUBS
    block = 4 * HALF
    smem = pl.BlockSpec(memory_space=pltpu.SMEM)
    vmem = pl.BlockSpec(memory_space=pltpu.VMEM)
    hbm = pl.BlockSpec(memory_space=pl.ANY)
    dma = pltpu.SemaphoreType.DMA
    normed, grads = pl.pallas_call(
        kernel,
        out_shape=(
            jax.ShapeDtypeStruct((seq_rows, model), BF),
            jax.ShapeDtypeStruct((slot_count, own_images, model), BF),
        ),
        in_specs=[smem] * 3 + [hbm] * 9,
        out_specs=(hbm, hbm),
        scratch_shapes=[
            pltpu.VMEM((hidden_width, hidden), BF),
            pltpu.VMEM((2, half_tail, hidden), BF),
            pltpu.VMEM((hidden, cols), BF),
            pltpu.VMEM((hidden, cols), BF),
            pltpu.VMEM((seq_rows, model), BF),
            pltpu.VMEM((seq_rows, model), BF),
            [pltpu.VMEM((2, n_ctx, 2, HALF, w), BF) for w in widths],
            [pltpu.VMEM((n_ctx, 2, HALF, w), BF) for w in widths * 2],
            [pltpu.VMEM((n_sec, HALF, w), BF) for w in widths * 2],
            [pltpu.VMEM((n_sec, HALF, w), BF) for w in widths * 2],
            [pltpu.VMEM((n_ctx, 2, n_sec * HALF, w), BF) for w in widths],
            pltpu.VMEM((2, own_images, slot_count, half_tail), BF),
            pltpu.VMEM((n_ctx, own_images, slot_count, half_tail), BF),
            pltpu.VMEM((n_sec, slot_count, half_tail), BF),
            pltpu.VMEM((n_sec, slot_count, half_tail), BF),
            pltpu.VMEM((2, 2, n_sec * HALF, half_tail), BF),
            pltpu.VMEM((2, n_sec * HALF, hidden), F32),
            pltpu.VMEM((2, SIDE, 2, 2 * HALF, hidden), BF),
            pltpu.VMEM((2, SIDE, 2, 2 * HALF, hidden), BF),
            pltpu.VMEM((RING, 2, SIDE, 2, 2 * HALF, TILE), F32),
            pltpu.VMEM((tiles, 2, 2, 2 * HALF, TILE), BF),
            pltpu.VMEM((tiles, 2, 2, 2 * HALF, TILE), BF),
            pltpu.VMEM((tiles, 2, 2, 2, 2 * HALF, TILE), BF),
            pltpu.VMEM((tiles, 2, 2, 2, 2 * HALF, TILE), BF),
            pltpu.VMEM((tiles, block, TILE), BF),
            pltpu.VMEM((pieces, block, TILE), BF),
            pltpu.VMEM((pieces, block, TILE), BF),
            pltpu.VMEM((seq_rows, model), BF),
            pltpu.VMEM((2, block, 128), F32),
            pltpu.VMEM((SUBS, n_ctx, 2, 2, HALF, wide), BF),
            [pltpu.VMEM((n_ctx, 2, 2, HALF, wide), BF)] * SUBS,
            pltpu.VMEM((SUBS, n_sec, 2, HALF, wide), BF),
            [pltpu.VMEM((n_sec, 2, HALF, wide), BF)] * SUBS,
            pltpu.VMEM((SUBS, n_ctx, slot_count, own_images, wide), BF),
            pltpu.VMEM((SUBS, slot_count, own_images, wide), BF),
            pltpu.VMEM(patches.shape, BF),
            pltpu.VMEM(patch_gain.shape, F32),
            pltpu.VMEM((hidden,), F32),
            pltpu.VMEM((model,), F32),
            pltpu.VMEM((model,), F32),
            pltpu.VMEM((1, patch_gain.shape[0]), F32),
            pltpu.VMEM((1, hidden), F32),
            pltpu.VMEM((1, model), F32),
            pltpu.VMEM((1, model), F32),
            pltpu.SMEM((6, n_sec), jnp.int32),
            dma((10 + SUBS + n_ctx,)),
            dma((4,)),
            dma((4,)),
            dma((4,)),
            dma((4,)),
            dma((2, 4)),
            dma((2, 4)),
            dma((2, 4)),
            dma((2, 4)),
            dma((SIDE, 4)),
            dma((SIDE, 4)),
            dma,
            dma,
            dma((2, 2)),
            dma((2, 2)),
            dma((2, 2)),
            dma((2, 2)),
            dma,
            dma,
            dma,
            dma,
            dma,
            dma,
            dma((2,)),
            dma((2,)),
            dma((tiles, 2)),
            dma((tiles, 2)),
            dma((tiles, 2)),
            dma((tiles, 2)),
            dma((tiles,)),
            dma((tiles,)),
            dma((SUBS,)),
            dma((SUBS,)),
            dma((SUBS,)),
            dma((SUBS,)),
            dma((SUBS,)),
            dma((SUBS,)),
        ],
        compiler_params=pltpu.CompilerParams(
            collective_id=0, has_side_effects=True, vmem_limit_bytes=63 << 20
        ),
        name="merger",
    )(
        img_seq,
        img_off,
        img_cnt,
        patches,
        patch_gain,
        b_merge_in,
        b_merge_out,
        norm_gain,
        w_merge_in,
        w_merge_out,
        text_embed[0],
        upstream[0],
    )
    normed, grads = hand_over(normed, grads)
    return (normed[None], grads)


def solution(mesh):
    placed = (
        P(None, ("sec", "ctx"), None),
        P(),
        P(None, "ctx"),
        P("ctx"),
        P("ctx", None),
        P(),
        P("sec", "ctx", None),
        P(),
        P("sec", "ctx", None),
        P(),
        P(),
        P(),
    )
    return jax.shard_map(
        local,
        mesh=mesh,
        in_specs=placed,
        out_specs=(P("sec", "ctx", None), P(None, ("sec", "ctx"), None)),
        check_vma=False,
    )
```
